256 devices in a mesh: dp: 32 (over z, x), mp: 8 (over y, core).
Axes of the slice: x: 4, y: 4, z: 8, core: 2. Of those that a mesh axis runs over, the one named last changes fastest.
Arguments:
- tokens: bfloat16 [32768, 8192], P(('dp', 'mp')), may hold values from -6 to 6
- key_value_weight: bfloat16 [8192, 2048], P(None, 'mp'), may hold values from -0.0625 to 0.0625
- adapter_down_weight: bfloat16 [64, 8192, 128], P(None, ('dp', 'mp')), may hold values from -0.0625 to 0.0625
- adapter_up_weight: bfloat16 [64, 64, 2048], P(None, 'dp', 'mp'), may hold values from -1 to 1
- adapter_per_request: int32 [128], replicated, may hold values from 0 to 63
- request_per_segment: int32 [256], replicated, may hold values from 0 to 127, never falling along the last dimension, each value on 1 to 4 neighbouring positions
Outputs:
- kv_out: bfloat16 [32768, 2048], P('dp', 'mp')
The draws below stay inside these ranges and needn't reach their ends.
Inputs may be any that keep to these rules, and one draw needn't show every extreme that they name: request_per_segment never falls along the segments; every request has 1 to 4 segments, one has exactly 4.
All inputs are finite; a program needn't handle non-finite values.
Results may differ from the reference program's by a relative error of at most 0.0043.
Values may be sent and summed in bfloat16 or wider, within the bound.
No kernel may reach another device: no remote copies, remote signals or barrier semaphores. Data moves between devices by JAX's collectives and lax.ppermute only.
A program may use at most 128 MiB of HBM per device.

```python
import math
import jax
import jax.numpy as jnp
import numpy as np
from jax import lax

MODEL_WIDTH = 8192
KEY_VALUE_WIDTH = 1024
ADAPTER_RANK = 64
SEG = 128
ADAPTER_TOTAL = 64
SEGS = 256
REQUESTS = 128
TOKENS = 32768


def plant(array, key, least, high):
    dims = array.shape
    place = [jax.random.randint(jax.random.fold_in(key, axis), (), 0, dims[axis]) for axis in range(len(dims))]
    array = array.at[tuple(place)].set(least)
    longest = dims.index(max(dims))
    place[longest] = (place[longest] + 1) % dims[longest]
    return array.at[tuple(place)].set(high)


def block_levels(own_key, dims, split, low, largest):
    loudness = 1.0
    for position, shards_of in split:
        heights = jax.random.uniform(jax.random.fold_in(jax.random.fold_in(own_key, 6), position), (shards_of,), jnp.float32, low / len(split), largest / len(split))
        loudness = loudness * jnp.repeat(jnp.exp(heights), dims[position] // shards_of).reshape((-1,) + (1,) * (len(dims) - 1 - position))
    return loudness


def rank_bounds(number_of, skew):
    portions = [(1 << 20) // math.isqrt(standing ** skew) + 1 for standing in range(1, number_of + 1)]
    scale = 1 + sum(portions) // (1 << 30)
    return np.cumsum(np.array([max(1, weight // scale) for weight in portions]))


def ranked(stream_key, extent, amount, slope):
    table = rank_bounds(amount, slope)
    lot = jax.random.randint(jax.random.fold_in(stream_key, 1), extent, 0, int(table[amount - 1]))
    standing = jnp.searchsorted(jnp.asarray(table, jnp.int32), lot, side="right")
    return jax.random.permutation(jax.random.fold_in(stream_key, 2), amount)[standing].astype(jnp.int32)


def profile(count, total, reach, slope):
    weights = [(1 << 20) // math.isqrt(standing ** slope) + 1 for standing in range(2, count + 1)]
    surplus, counts = total - reach - (count - 1), [1] * (count - 1)
    while surplus > 0:
        candidates = [i for i in range(count - 1) if counts[i] < reach]
        whole, remaining = sum([weights[i] for i in candidates]), surplus
        for i in candidates:
            addition = min(reach - counts[i], max(1, remaining * weights[i] // whole), surplus)
            counts[i] = counts[i] + addition
            surplus = surplus - addition
    return np.array([reach] + counts)


def uneven(stream_key, number_of, total, bound, slope):
    if number_of == 2:
        one = jax.random.randint(stream_key, (), max(1, total - bound), min(bound, total - 1) + 1)
        return jnp.stack([one, total - one])
    tallies = jnp.asarray(profile(number_of, total, bound, slope), jnp.int32)
    twos = (number_of - 1) // 2
    donor, sink = tallies[1:1 + 2 * twos:2], tallies[2:2 + 2 * twos:2]
    room = jnp.minimum(donor - 1, bound - sink)
    passed = jax.random.randint(jax.random.fold_in(stream_key, 1), (twos,), 0, 1 << 20) % (room + 1)
    tallies = tallies.at[1:1 + 2 * twos:2].set(donor - passed).at[2:2 + 2 * twos:2].set(sink + passed)
    return tallies[jax.random.permutation(jax.random.fold_in(stream_key, 2), number_of)]


def scatter_about(key, shape, spread, bound, cuts=(), kind=jnp.bfloat16):
    level = block_levels(key, shape, cuts, -0.22, 0.18) if cuts else 1.0
    entries = jax.random.normal(key, shape, jnp.float32) * spread * level
    return jnp.minimum(jnp.maximum(entries, -bound), bound).astype(kind)


def setup_inputs(seed: int = 0) -> dict:
    seeds = jax.random.split(jax.random.key(seed), 7)
    return {
        "tokens": scatter_about(seeds[0], (TOKENS, MODEL_WIDTH), 1.0, 6.0, ((0, 256),)),
        "key_value_weight": scatter_about(seeds[1], (MODEL_WIDTH, 2 * KEY_VALUE_WIDTH), MODEL_WIDTH ** -0.5, 0.0625, ((1, 8),)),
        "adapter_down_weight": scatter_about(seeds[2], (ADAPTER_TOTAL, MODEL_WIDTH, 2 * ADAPTER_RANK), MODEL_WIDTH ** -0.5, 0.0625, ((1, 256),)),
        "adapter_up_weight": scatter_about(seeds[3], (ADAPTER_TOTAL, ADAPTER_RANK, 2 * KEY_VALUE_WIDTH), (ADAPTER_RANK // 2) ** -0.5, 1.0, ((1, 32), (2, 8))),
        "adapter_per_request": plant(ranked(seeds[4], (REQUESTS,), ADAPTER_TOTAL, 2), jax.random.fold_in(seeds[4], 3), 0, ADAPTER_TOTAL - 1).astype(jnp.int32),
        "request_per_segment": jnp.searchsorted(jnp.cumsum(uneven(seeds[5], REQUESTS, SEGS, 4, 2)), jnp.arange(SEGS), side="right").astype(jnp.int32),
    }


def reference(tokens, key_value_weight, adapter_down_weight, adapter_up_weight, adapter_per_request, request_per_segment):
    seg_adapter = jnp.take(adapter_per_request, request_per_segment, axis=0).astype(jnp.int32)
    base = jnp.dot(tokens, key_value_weight, preferred_element_type=jnp.float32)
    count = request_per_segment.shape[0]
    partial_outputs = tokens.reshape(count, SEG, MODEL_WIDTH)

    def one_segment(position_index):
        adapter_choice = seg_adapter[position_index]
        rank_output = jnp.dot(partial_outputs[position_index], adapter_down_weight[adapter_choice], preferred_element_type=jnp.float32).astype(jnp.bfloat16)
        selected_up_weight = adapter_up_weight[adapter_choice]
        key_part = jnp.dot(rank_output[:, :ADAPTER_RANK], selected_up_weight[:, :KEY_VALUE_WIDTH], preferred_element_type=jnp.float32)
        value_part = jnp.dot(rank_output[:, ADAPTER_RANK:], selected_up_weight[:, KEY_VALUE_WIDTH:], preferred_element_type=jnp.float32)
        return jnp.concatenate([key_part, value_part], axis=1)

    delta = lax.map(one_segment, jnp.arange(count, dtype=jnp.int32))
    return (base + delta.reshape(count * SEG, 2 * KEY_VALUE_WIDTH)).astype(jnp.bfloat16)
```

```python
import functools

import jax
import jax.numpy as jnp
from jax import lax
from jax.experimental import pallas as pl
from jax.experimental.pallas import tpu as pltpu
from jax.sharding import Mesh
from jax.sharding import PartitionSpec as P

NZ, NX, NY, NC = 8, 4, 4, 2
NDP = NZ * NX
SEG = 128
K = 8192
RANK = 64
COLS = 256
KQ = K // NY
BF16, F32 = jnp.bfloat16, jnp.float32
VMEM_LIMIT = 48 * 1024 * 1024


def params(**kw):
    return pltpu.CompilerParams(vmem_limit_bytes=VMEM_LIMIT, **kw)


def cost(flops, nbytes):
    return pl.CostEstimate(flops=flops, bytes_accessed=nbytes, transcendentals=0)


def shift(x, axis, by):
    n = {"y": NY, "c": NC}[axis]
    return lax.ppermute(x, axis, [(i, (i + by) % n) for i in range(n)])


def pack_kernel(apr, rps, down_ref, up_ref, out_ref):
    row = lax.broadcasted_iota(jnp.int32, (8, 128), 0)

    def to_device(n, carry):
        first = (n // NC) * (NY * NC) + n % NC
        ids = [apr[rps[first + s * NC]] for s in range(NY)]
        for s in range(NY):
            out_ref[n, 32 * s : 32 * s + 32, :] = down_ref[ids[s]]
        ups = [
            jnp.where(row < 4, up_ref[ids[s]], up_ref[ids[s + 1]]) for s in (0, 2)
        ]
        out_ref[n, 128:144, :] = jnp.concatenate(ups, axis=0).astype(BF16)
        return carry

    lax.fori_loop(0, NDP * NC, to_device, 0, unroll=4)


def pack(apr, rps, down, up_twice):
    return pl.pallas_call(
        pack_kernel,
        grid_spec=pltpu.PrefetchScalarGridSpec(
            num_scalar_prefetch=2,
            grid=(1,),
            in_specs=[
                pl.BlockSpec((64, 32, 128), lambda i, *_: (0, 0, 0)),
                pl.BlockSpec((64, 8, 128), lambda i, *_: (0, 0, 0)),
            ],
            out_specs=pl.BlockSpec((64, 144, 128), lambda i, *_: (0, 0, 0)),
        ),
        out_shape=jax.ShapeDtypeStruct((64, 144, 128), BF16),
        compiler_params=params(),
        cost_estimate=cost(0, 3 << 20),
    )(apr, rps, down, up_twice)


def quarter_of(x_ref, q, pair):
    at = pair * 512 + (q // 2) * 128
    a = x_ref[:, pl.ds(pl.multiple_of(at, 128), 128)]
    b = x_ref[:, pl.ds(pl.multiple_of(at + 256, 128), 128)]
    low = jnp.concatenate([a[:, :64], b[:, :64]], axis=1)
    high = jnp.concatenate([a[:, 64:], b[:, 64:]], axis=1)
    return jnp.where(q % 2 == 0, low, high)


def split_kernel(first, x_ref, *outs):
    for pair in range(16):
        lanes = slice(128 * pair, 128 * pair + 128)
        for i in range(NY):
            q = (first[0] + i) % NY
            part = quarter_of(x_ref, q, pair)
            if i == 0:
                outs[0][:, lanes] = part
            elif i < 3:
                outs[1][i - 1, :, lanes] = part
            else:
                outs[2][:, lanes] = part


def split_quarters(x, first):
    rows = x.shape[0]
    return pl.pallas_call(
        split_kernel,
        grid_spec=pltpu.PrefetchScalarGridSpec(
            num_scalar_prefetch=1,
            grid=(1,),
            in_specs=[pl.BlockSpec((rows, K), lambda i, *_: (0, 0))],
            out_specs=[
                pl.BlockSpec((rows, KQ), lambda i, *_: (0, 0)),
                pl.BlockSpec((2, rows, KQ), lambda i, *_: (0, 0, 0)),
                pl.BlockSpec((rows, KQ), lambda i, *_: (0, 0)),
            ],
        ),
        out_shape=[
            jax.ShapeDtypeStruct((rows, KQ), BF16),
            jax.ShapeDtypeStruct((2, rows, KQ), BF16),
            jax.ShapeDtypeStruct((rows, KQ), BF16),
        ],
        compiler_params=params(),
        cost_estimate=cost(0, 4 * rows * K),
    )(first, x)


def own_quarter_kernel(y, x0, a_lo, a_hi, b_lo, b_hi, out):
    q = y[0]
    for pair in range(16):
        lanes = slice(128 * pair, 128 * pair + 128)
        out[0, :, lanes] = quarter_of(x0, q, pair)
        out[1, 0:64, lanes] = quarter_of(b_lo, q, pair)
        out[1, 64:128, lanes] = quarter_of(b_hi, q, pair)
        out[2, 0:64, lanes] = quarter_of(a_lo, q, pair)
        out[2, 64:128, lanes] = quarter_of(a_hi, q, pair)


def own_quarter(y, x0, a_lo, a_hi, b_lo, b_hi):
    half = pl.BlockSpec((64, K), lambda i, *_: (0, 0))
    return pl.pallas_call(
        own_quarter_kernel,
        grid_spec=pltpu.PrefetchScalarGridSpec(
            num_scalar_prefetch=1,
            grid=(1,),
            in_specs=[pl.BlockSpec((128, K), lambda i, *_: (0, 0))] + [half] * 4,
            out_specs=pl.BlockSpec((3, 128, KQ), lambda i, *_: (0, 0, 0)),
        ),
        out_shape=jax.ShapeDtypeStruct((3, 128, KQ), BF16),
        compiler_params=params(),
        cost_estimate=cost(0, 8 << 20),
    )(y, x0, a_lo, a_hi, b_lo, b_hi)


def low_kernel(y, x_ref, far_lo, far_hi, down_ref, *rest):
    outs, sums = rest[:NY], rest[NY]
    me = y[0]
    for d in range(NY):
        s = (me + d) % NY
        factor = down_ref[:, pl.ds(pl.multiple_of(32 * s, 32), 32), :].reshape(KQ, 128)
        if d == 2:
            x = jnp.concatenate([far_lo[...], far_hi[...]], axis=0)
        else:
            x = x_ref[{0: 0, 1: 1, 3: 2}[d]]
        sums[s] = jnp.dot(x, factor, preferred_element_type=F32)
    lane = lax.broadcasted_iota(jnp.int32, (128, 128), 1)
    for e in range(NY):
        value = (me + e) % NY >= NY // 2
        for pair in range(2):
            a, b = sums[2 * pair], sums[2 * pair + 1]
            keys = jnp.where(lane < 64, a, pltpu.roll(b, 64, 1))
            values = jnp.where(lane < 64, pltpu.roll(a, 64, 1), b)
            outs[e][128 * pair : 128 * pair + 128, :] = jnp.where(value, values, keys)


def low_parts(y, x, far_lo, far_hi, recv):
    quarter = pl.BlockSpec((64, KQ), lambda i, *_: (0, 0))
    return pl.pallas_call(
        low_kernel,
        grid_spec=pltpu.PrefetchScalarGridSpec(
            num_scalar_prefetch=1,
            grid=(1,),
            in_specs=[
                pl.BlockSpec((3, 128, KQ), lambda i, *_: (0, 0, 0)),
                quarter,
                quarter,
                pl.BlockSpec((64, 128, 128), lambda i, *_: (0, 0, 0)),
            ],
            out_specs=[pl.BlockSpec((256, 128), lambda i, *_: (0, 0))] * NY,
            scratch_shapes=[pltpu.VMEM((NY, 128, 128), F32)],
        ),
        out_shape=[jax.ShapeDtypeStruct((256, 128), F32)] * NY,
        compiler_params=params(),
        cost_estimate=cost(2 * 512 * KQ * 128, 5 << 20),
    )(y, x, far_lo, far_hi, recv)


def up_kernel(recv_ref, out_ref):
    r = lax.broadcasted_iota(jnp.int32, (512, 512), 0)
    k = lax.broadcasted_iota(jnp.int32, (512, 512), 1)
    pair, half, seg, rank = r // 256, (r // 128) % 2, (r // 64) % 2, r % 64
    source = (rank // 2) * 16 + (pair * 2 + seg) * 4 + (rank % 2) * 2 + half
    order = (k == source).astype(F32).astype(BF16)
    every = recv_ref[...].reshape(NDP, NC, 16, 128)
    for c in range(NC):
        rows = every[:, c].reshape(512, 128)
        got = jnp.dot(order, rows, preferred_element_type=F32).astype(BF16)
        for p in range(2):
            for h in range(2):
                at = 256 * p + 128 * h
                out_ref[c, p, :, 128 * h : 128 * h + 128] = got[at : at + 128]


def up_rows(recv):
    return pl.pallas_call(
        up_kernel,
        grid=(1,),
        in_specs=[pl.BlockSpec((64, 16, 128), lambda i: (0, 8, 0))],
        out_specs=pl.BlockSpec((NC, 2, 128, COLS), lambda i: (0, 0, 0, 0)),
        out_shape=jax.ShapeDtypeStruct((NC, 2, 128, COLS), BF16),
        compiler_params=params(),
        cost_estimate=cost(2 * 512 * 512 * 256, 1 << 19),
    )(recv)


def near_kernel(x0, a_lo, a_hi, b_lo, b_hi, w0, w1, out):
    @pl.when(pl.program_id(0) == 0)
    def _():
        out[...] = jnp.zeros_like(out)

    x = jnp.concatenate([x0[...], b_lo[...], b_hi[...], a_lo[...], a_hi[...]], axis=0)
    out[:, :COLS] += jnp.dot(x, w0[...], preferred_element_type=F32)
    out[:, COLS:] += jnp.dot(x, w1[...], preferred_element_type=F32)


def near_base(x0, a_lo, a_hi, b_lo, b_hi, w0, w1):
    step = 1024
    half = pl.BlockSpec((64, step), lambda i: (0, i))
    weight = pl.BlockSpec((step, COLS), lambda i: (i, 0))
    return pl.pallas_call(
        near_kernel,
        grid=(K // step,),
        in_specs=[pl.BlockSpec((128, step), lambda i: (0, i))] + [half] * 4 + [weight] * 2,
        out_specs=pl.BlockSpec((384, 512), lambda i: (0, 0)),
        out_shape=jax.ShapeDtypeStruct((384, 512), F32),
        compiler_params=params(),
        cost_estimate=cost(2 * 384 * K * 512, 15 << 20),
    )(x0, a_lo, a_hi, b_lo, b_hi, w0, w1)


def quarter_weight(offset):
    return pl.BlockSpec(
        (8, None, 64, COLS), lambda i, y: (i % 4, (y[0] + offset(i // 4)) % NY, 0, 0)
    )


def far_kernel(y, lo0, hi0, lo1, hi1, w0, w1, out):
    i = pl.program_id(0)

    @pl.when(i == 0)
    def _():
        out[...] = jnp.zeros_like(out)

    lo = jnp.where(i < 4, lo0[...], lo1[...])
    hi = jnp.where(i < 4, hi0[...], hi1[...])
    x = jnp.concatenate([lo, hi], axis=0)
    out[:, :COLS] += jnp.dot(x, w0[...].reshape(512, COLS), preferred_element_type=F32)
    out[:, COLS:] += jnp.dot(x, w1[...].reshape(512, COLS), preferred_element_type=F32)


def far_base(y, lo0, hi0, lo1, hi1, w0, w1):
    first = pl.BlockSpec((64, 512), lambda i, y: (0, jnp.minimum(i, 3)))
    then = pl.BlockSpec(
        (None, 64, 512),
        lambda i, y: (jnp.maximum(i - 4, 0) // 4, 0, jnp.maximum(i - 4, 0) % 4),
    )
    weight = quarter_weight(lambda j: j)
    return pl.pallas_call(
        far_kernel,
        grid_spec=pltpu.PrefetchScalarGridSpec(
            num_scalar_prefetch=1,
            grid=(12,),
            in_specs=[first, first, then, then, weight, weight],
            out_specs=pl.BlockSpec((128, 512), lambda i, y: (0, 0)),
        ),
        out_shape=jax.ShapeDtypeStruct((128, 512), F32),
        compiler_params=params(),
        cost_estimate=cost(2 * 128 * 3 * KQ * 512, 8 << 20),
    )(y, lo0, hi0, lo1, hi1, w0, w1)


def last_kernel(yc, lo, hi, w0, w1, near, far, p0, p1, p2, p3, up, out, out_partner, total):
    i = pl.program_id(0)
    me, core = yc[0], yc[1]

    @pl.when(i == 0)
    def _():
        total[...] = far[...]

    x = jnp.concatenate([lo[...], hi[...]], axis=0)
    total[:, :COLS] += jnp.dot(x, w0[...].reshape(512, COLS), preferred_element_type=F32)
    total[:, COLS:] += jnp.dot(x, w1[...].reshape(512, COLS), preferred_element_type=F32)

    @pl.when(i == 3)
    def _():
        low = (p0[...] + p1[...] + p2[...] + p3[...]).astype(BF16).astype(F32)
        left = lax.broadcasted_iota(jnp.int32, (128, 128), 1) < 64
        for d in range(NY):
            s = (me + d) % NY
            pair = s // 2
            both = jnp.where(pair == 0, low[:128], low[128:])
            mine = jnp.where(left == (s % 2 == 0), both, 0.0).astype(BF16)
            if d == 2:
                base = total[...]
            else:
                at = {0: 0, 1: 128, 3: 256}[d]
                base = near[at : at + 128, :]
            own = jnp.dot(mine, up[core, pair], preferred_element_type=F32)
            other = jnp.dot(mine, up[1 - core, pair], preferred_element_type=F32)
            out[s, core] = (base[:, :COLS] + own).astype(BF16)
            out_partner[s] = (base[:, COLS:] + other).astype(BF16)


def last(yc, lo, hi, w0, w1, near, far, parts, up):
    quarter = pl.BlockSpec((64, 512), lambda i, y: (0, i))
    weight = quarter_weight(lambda j: 3)

    def whole(*shape):
        return pl.BlockSpec(shape, lambda i, y: (0,) * len(shape))

    return pl.pallas_call(
        last_kernel,
        grid_spec=pltpu.PrefetchScalarGridSpec(
            num_scalar_prefetch=1,
            grid=(4,),
            in_specs=[quarter, quarter, weight, weight, whole(384, 512), whole(128, 512)]
            + [whole(256, 128)] * 4
            + [whole(NC, 2, 128, COLS)],
            out_specs=[whole(NY, NC, 128, COLS), whole(NY, 128, COLS)],
            scratch_shapes=[pltpu.VMEM((128, 512), F32)],
        ),
        out_shape=[
            jax.ShapeDtypeStruct((NY, NC, 128, COLS), BF16),
            jax.ShapeDtypeStruct((NY, 128, COLS), BF16),
        ],
        compiler_params=params(),
        cost_estimate=cost(2 * 128 * KQ * 512, 6 << 20),
    )(yc, lo, hi, w0, w1, near, far, *parts, up)


def on_device(tokens, weight, down, up, apr, rps):
    y, c = lax.axis_index("y"), lax.axis_index("c")
    yv = y.reshape(1).astype(jnp.int32)
    yc = jnp.stack([y, c]).astype(jnp.int32)

    lo, hi = tokens[:64], tokens[64:]
    a_lo, b_hi = shift(lo, "y", 1), shift(hi, "y", -1)
    a_hi, b_lo = shift(hi, "y", 1), shift(lo, "y", -1)

    rows = up.reshape(64, 4, 128).astype(F32)
    send = pack(apr, rps, down, jnp.concatenate([rows, rows], axis=1))
    recv = lax.all_to_all(send, ("z", "x", "c"), 0, 0)
    partner_weight = shift(weight, "c", 1)

    lo0, lo12, lo3 = [shift(v, "y", 1) for v in split_quarters(a_lo, (yv + 1) % NY)]
    hi0, hi12, hi3 = [shift(v, "y", -1) for v in split_quarters(b_hi, (yv + 3) % NY)]

    mine = own_quarter(yv, tokens, a_lo, a_hi, b_lo, b_hi)
    near = near_base(tokens, a_lo, a_hi, b_lo, b_hi, weight, partner_weight)
    w0 = weight.reshape(32, NY, 64, COLS)
    w1 = partner_weight.reshape(32, NY, 64, COLS)

    parts = low_parts(yv, mine, lo0, hi0, recv)
    parts = [parts[0]] + [shift(parts[e], "y", e) for e in (1, 2, 3)]
    up_sorted = up_rows(recv)
    far = far_base(yv, lo0, hi0, lo12, hi12, w0, w1)
    out, out_partner = last(yc, lo3, hi3, w0, w1, near, far, parts, up_sorted)
    theirs = shift(out_partner, "c", 1)
    zero = jnp.zeros((), jnp.int32)
    out = lax.dynamic_update_slice(
        out, theirs[:, None], (zero, (1 - c).astype(jnp.int32), zero, zero)
    )
    return out.reshape(NY * NC * 128, COLS)


def solution(mesh):
    axes = Mesh(mesh.devices.reshape(NZ, NX, NY, NC), ("z", "x", "y", "c"))
    every = ("z", "x", "y", "c")
    placed = (
        P(every, None),
        P(None, ("y", "c")),
        P(None, every, None),
        P(None, ("z", "x"), ("y", "c")),
        P(),
        P(),
    )
    return jax.shard_map(
        on_device,
        mesh=axes,
        in_specs=placed,
        out_specs=P(("z", "x"), ("y", "c")),
        check_vma=False,
    )
```

```python
import functools

import jax
import jax.numpy as jnp
from jax import lax
from jax.experimental import pallas as pl
from jax.experimental.pallas import tpu as pltpu
from jax.sharding import Mesh
from jax.sharding import PartitionSpec as P

NZ, NX, NY, NC = 8, 4, 4, 2
NDP = NZ * NX
SEG = 128
K = 8192
RANK = 64
COLS = 256
KQ = K // NY
BF16, F32 = jnp.bfloat16, jnp.float32
VMEM_LIMIT = 20 * 1024 * 1024
PACK = 32
STEP = 2048
AHEAD = 10**11


def params(**kw):
    return pltpu.CompilerParams(vmem_limit_bytes=VMEM_LIMIT, **kw)


def cost(flops, nbytes):
    return pl.CostEstimate(flops=flops, bytes_accessed=nbytes, transcendentals=0)


def in_hbm(x):
    return pltpu.with_memory_space_constraint(x, pltpu.HBM)


def shift(x, axis, by):
    n = {"y": NY, "c": NC}[axis]
    return lax.ppermute(x, axis, [(i, (i + by) % n) for i in range(n)])


def around(x, to_same_core=True):
    pairs = []
    for y in range(NY):
        for c in range(NC):
            to = (y + 1 - 2 * c) % NY
            pairs.append((y * NC + c, to * NC + (c if to_same_core else 1 - c)))
    return lax.ppermute(x, ("y", "c"), pairs)


def pack_kernel(apr, rps, down_ref, up_ref, out_ref, table):
    step = pl.program_id(0)

    @pl.when(step == 0)
    def _():
        def fill(a, carry):
            v = up_ref[a].astype(F32)
            table[a] = jnp.concatenate([v[:, :128], v[:, 128:]] * 2, axis=0)
            return carry

        lax.fori_loop(0, 64, fill, 0, unroll=8)

    row = lax.broadcasted_iota(jnp.int32, (8, 128), 0)

    def to_device(n, carry):
        first = (step * PACK + n) // NC * (NY * NC) + n % NC
        ids = [apr[rps[first + s * NC]] for s in range(NY)]
        for s in range(NY):
            out_ref[n, 32 * s : 32 * s + 32, :] = down_ref[ids[s]]
        ups = [jnp.where(row < 4, table[ids[s]], table[ids[s + 1]]) for s in (0, 2)]
        out_ref[n, 128:144, :] = jnp.concatenate(ups, axis=0).astype(BF16)
        return carry

    lax.fori_loop(0, PACK, to_device, 0, unroll=8)


def pack(apr, rps, down, up):
    return pl.pallas_call(
        pack_kernel,
        grid_spec=pltpu.PrefetchScalarGridSpec(
            num_scalar_prefetch=2,
            grid=(NDP * NC // PACK,),
            in_specs=[
                pl.BlockSpec((64, 32, 128), lambda i, *_: (0, 0, 0)),
                pl.BlockSpec((64, 2, COLS), lambda i, *_: (0, 0, 0)),
            ],
            out_specs=pl.BlockSpec((PACK, 144, 128), lambda i, *_: (i, 0, 0)),
            scratch_shapes=[pltpu.VMEM((64, 8, 128), F32)],
        ),
        out_shape=jax.ShapeDtypeStruct((NDP * NC, 144, 128), BF16),
        compiler_params=pltpu.CompilerParams(vmem_limit_bytes=60 * 1024 * 1024),
        cost_estimate=cost(0, 3 << 20),
    )(apr, rps, down, up)


def quarter_of(x_ref, q, pair):
    at = pair * 512 + (q // 2) * 128
    a = x_ref[:, pl.ds(pl.multiple_of(at, 128), 128)]
    b = x_ref[:, pl.ds(pl.multiple_of(at + 256, 128), 128)]
    low = jnp.concatenate([a[:, :64], b[:, :64]], axis=1)
    high = jnp.concatenate([a[:, 64:], b[:, 64:]], axis=1)
    return jnp.where(q % 2 == 0, low, high)


def split_kernel(first, x_ref, *outs):
    for pair in range(16):
        lanes = slice(128 * pair, 128 * pair + 128)
        for i in range(NY):
            outs[i][:, lanes] = quarter_of(x_ref, (first[0] + i) % NY, pair)


def split_quarters(first, x):
    return pl.pallas_call(
        split_kernel,
        grid_spec=pltpu.PrefetchScalarGridSpec(
            num_scalar_prefetch=1,
            grid=(1,),
            in_specs=[pl.BlockSpec((SEG, K), lambda i, *_: (0, 0))],
            out_specs=[pl.BlockSpec((SEG, KQ), lambda i, *_: (0, 0))] * NY,
        ),
        out_shape=[jax.ShapeDtypeStruct((SEG, KQ), BF16)] * NY,
        compiler_params=params(),
        cost_estimate=cost(AHEAD, 4 * SEG * K),
    )(first, x)


def low_kernel(yc, own, near, other, far, down_ref, after, *rest):
    outs, sums = rest[:NY], rest[NY]
    me, core = yc[0], yc[1]
    for x, d in zip((own, near, other, far), (0, 3 - 2 * core, 1 + 2 * core, 2)):
        s = (me + d) % NY
        factor = down_ref[:, pl.ds(pl.multiple_of(32 * s, 32), 32), :].reshape(KQ, 128)
        sums[s] = jnp.dot(x[...], factor, preferred_element_type=F32)
    lane = lax.broadcasted_iota(jnp.int32, (128, 128), 1)
    for e in range(NY):
        value = (me + e) % NY >= NY // 2
        for pair in range(2):
            a, b = sums[2 * pair], sums[2 * pair + 1]
            keys = jnp.where(lane < 64, a, pltpu.roll(b, 64, 1))
            values = jnp.where(lane < 64, pltpu.roll(a, 64, 1), b)
            outs[e][128 * pair : 128 * pair + 128, :] = jnp.where(value, values, keys)


def low_parts(yc, quarters, recv, after):
    return pl.pallas_call(
        low_kernel,
        grid_spec=pltpu.PrefetchScalarGridSpec(
            num_scalar_prefetch=1,
            grid=(1,),
            in_specs=[pl.BlockSpec((SEG, KQ), lambda i, *_: (0, 0))] * 4
            + [
                pl.BlockSpec((64, 128, 128), lambda i, *_: (0, 0, 0)),
                pl.BlockSpec(memory_space=pl.ANY),
            ],
            out_specs=[pl.BlockSpec((256, 128), lambda i, *_: (0, 0))] * NY,
            scratch_shapes=[pltpu.VMEM((NY, 128, 128), F32)],
        ),
        out_shape=[jax.ShapeDtypeStruct((256, 128), F32)] * NY,
        compiler_params=params(),
        cost_estimate=cost(2 * 512 * KQ * 128, 5 << 20),
    )(yc, *[in_hbm(q) for q in quarters], recv, after)


def up_kernel(recv_ref, out_ref):
    r = lax.broadcasted_iota(jnp.int32, (512, 512), 0)
    k = lax.broadcasted_iota(jnp.int32, (512, 512), 1)
    pair, half, seg, rank = r // 256, (r // 128) % 2, (r // 64) % 2, r % 64
    source = (rank // 2) * 16 + (pair * 2 + seg) * 4 + half * 2 + rank % 2
    order = (k == source).astype(F32).astype(BF16)
    every = recv_ref[...].reshape(NDP, NC, 16, 128)
    for c in range(NC):
        rows = every[:, c].reshape(512, 128)
        got = jnp.dot(order, rows, preferred_element_type=F32).astype(BF16)
        for p in range(2):
            for h in range(2):
                at = 256 * p + 128 * h
                out_ref[c, p, :, 128 * h : 128 * h + 128] = got[at : at + 128]


def up_rows(recv):
    return pl.pallas_call(
        up_kernel,
        grid=(1,),
        in_specs=[pl.BlockSpec((64, 16, 128), lambda i: (0, 8, 0))],
        out_specs=pl.BlockSpec((NC, 2, 128, COLS), lambda i: (0, 0, 0, 0)),
        out_shape=jax.ShapeDtypeStruct((NC, 2, 128, COLS), BF16),
        compiler_params=params(),
        cost_estimate=cost(2 * 512 * 512 * 256, 1 << 19),
    )(recv)


def near_kernel(n, yc, *refs):
    xs, (w0, w1) = refs[:n], refs[n : n + 2]
    out, quarters = refs[-n - 1], refs[-n:]

    @pl.when(pl.program_id(0) == 0)
    def _():
        out[...] = jnp.zeros_like(out)

    for x, quarter in zip(xs, quarters):
        for pair in range(STEP // 512):
            quarter[:, 128 * pair : 128 * pair + 128] = quarter_of(x, yc[0], pair)
    x = jnp.concatenate([x[...] for x in xs], axis=0)
    out[:, :COLS] += jnp.dot(x, w0[...], preferred_element_type=F32)
    out[:, COLS:] += jnp.dot(x, w1[...], preferred_element_type=F32)


def near_base(yc, xs, w0, w1, after=()):
    step, n = STEP, len(xs)
    weight = pl.BlockSpec((step, COLS), lambda i, yc: (i, 0))
    result = pl.pallas_call(
        functools.partial(near_kernel, n),
        grid_spec=pltpu.PrefetchScalarGridSpec(
            num_scalar_prefetch=1,
            grid=(K // step,),
            in_specs=[pl.BlockSpec((SEG, step), lambda i, yc: (0, i))] * n
            + [weight] * 2
            + [pl.BlockSpec(memory_space=pl.ANY)] * len(after),
            out_specs=[pl.BlockSpec((SEG * n, 2 * COLS), lambda i, yc: (0, 0))]
            + [pl.BlockSpec((SEG, step // NY), lambda i, yc: (0, i))] * n,
        ),
        out_shape=[jax.ShapeDtypeStruct((SEG * n, 2 * COLS), F32)]
        + [jax.ShapeDtypeStruct((SEG, KQ), BF16)] * n,
        compiler_params=params(),
        cost_estimate=cost(2 * SEG * n * K * 512, 12 << 20),
    )(yc, *xs, w0, w1, *after)
    return result[0], result[1:]


def quarter_weight(offset):
    return pl.BlockSpec((32, None, 64, COLS), lambda i, yc: (0, (yc[0] + offset(i)) % NY, 0, 0))


def far_kernel(adds, yc, *refs):
    *xs, w0, w1, before, out = refs
    i = pl.program_id(0)

    @pl.when(i == 0)
    def _():
        out[...] = before[...] if adds else jnp.zeros_like(out)

    x = xs[0][...]
    for j in range(1, len(xs)):
        x = jnp.where(i == j, xs[j][...], x)
    out[:, :COLS] += jnp.dot(x, w0[...].reshape(KQ, COLS), preferred_element_type=F32)
    out[:, COLS:] += jnp.dot(x, w1[...].reshape(KQ, COLS), preferred_element_type=F32)


def far_base(yc, xs, start, w0, w1, before, adds):
    weight = quarter_weight(lambda i: start + i)
    n = len(xs)
    return pl.pallas_call(
        functools.partial(far_kernel, adds),
        grid_spec=pltpu.PrefetchScalarGridSpec(
            num_scalar_prefetch=1,
            grid=(n,),
            in_specs=[pl.BlockSpec((SEG, KQ), lambda i, yc: (0, 0))] * n
            + [weight] * 2
            + [whole(SEG, 512) if adds else pl.BlockSpec(memory_space=pl.ANY)],
            out_specs=pl.BlockSpec((SEG, 512), lambda i, yc: (0, 0)),
        ),
        out_shape=jax.ShapeDtypeStruct((SEG, 512), F32),
        compiler_params=params(),
        cost_estimate=cost(2 * SEG * n * KQ * 512, n * (3 << 20)),
    )(yc, *xs, w0, w1, before)


def whole(*shape):
    return pl.BlockSpec(shape, lambda i, yc: (0,) * len(shape))


def sum_kernel(yc, first, second, far, p0, p1, p2, p3, up, out, out_partner):
    me, core = yc[0], yc[1]
    low = (p0[...] + p1[...] + p2[...] + p3[...]).astype(BF16).astype(F32)
    left = lax.broadcasted_iota(jnp.int32, (128, 128), 1) < 64
    bases = (first[:SEG, :], first[SEG:, :], second[...], far[...])
    for d, base in zip((0, 3 - 2 * core, 1 + 2 * core, 2), bases):
        s = (me + d) & 3
        both = jnp.where(s < 2, low[:SEG], low[SEG:])
        mine = jnp.where(left == (s & 1 == 0), both, 0.0).astype(BF16)
        own = jnp.dot(mine, up[core, s // 2], preferred_element_type=F32)
        other = jnp.dot(mine, up[1 - core, s // 2], preferred_element_type=F32)
        out[s] = (base[:, :COLS] + own).astype(BF16)
        out_partner[s] = (base[:, COLS:] + other).astype(BF16)


def sum_up(yc, first, second, far, parts, up):
    return pl.pallas_call(
        sum_kernel,
        grid_spec=pltpu.PrefetchScalarGridSpec(
            num_scalar_prefetch=1,
            grid=(1,),
            in_specs=[whole(2 * SEG, 512), whole(SEG, 512), whole(SEG, 512)]
            + [whole(256, 128)] * NY
            + [whole(NC, 2, 128, COLS)],
            out_specs=[
                pl.BlockSpec((NY, None, SEG, COLS), lambda i, yc: (0, yc[1], 0, 0)),
                whole(NY, SEG, COLS),
            ],
        ),
        out_shape=[
            jax.ShapeDtypeStruct((NY, NC, SEG, COLS), BF16),
            jax.ShapeDtypeStruct((NY, SEG, COLS), BF16),
        ],
        compiler_params=params(),
        cost_estimate=cost(2 * 512 * 128 * 512, 3 << 20),
    )(yc, first, second, far, *parts, up)


def on_device(tokens, weight, down, up, apr, rps):
    y, c = lax.axis_index("y"), lax.axis_index("c")
    yc = jnp.stack([y, c]).astype(jnp.int32)

    near = around(tokens)
    partner_tokens = shift(tokens, "c", 1)
    other = around(partner_tokens, False)
    ahead = ((y + 1 - 2 * c + NY) & 3).reshape(1).astype(jnp.int32)
    q0, q1, q2, q3 = [around(v) for v in split_quarters(ahead, near)]

    send = pack(apr, rps, down, up)
    recv = lax.all_to_all(send, ("z", "x", "c"), 0, 0)
    partner_weight = shift(weight, "c", 1)

    w0 = weight.reshape(32, NY, 64, COLS)
    w1 = partner_weight.reshape(32, NY, 64, COLS)
    first, quarters = near_base(yc, [tokens, near], weight, partner_weight)
    second, more = near_base(yc, [other], weight, partner_weight, (first,))
    far = far_base(yc, [q0, q1, q2], 0, w0, w1, second, False)

    parts = low_parts(yc, [*quarters, *more, q0], recv, far)
    far = far_base(yc, [q3], 3, w0, w1, far, True)
    parts = [parts[0]] + [shift(parts[e], "y", e) for e in (1, 2, 3)]
    up_sorted = up_rows(recv)
    out, out_partner = sum_up(yc, first, second, far, parts, up_sorted)
    theirs = shift(out_partner, "c", 1)
    zero = jnp.zeros((), jnp.int32)
    out = lax.dynamic_update_slice(
        out, theirs[:, None], (zero, (1 - c).astype(jnp.int32), zero, zero)
    )
    return out.reshape(NY * NC * SEG, COLS)


def solution(mesh):
    axes = Mesh(mesh.devices.reshape(NZ, NX, NY, NC), ("z", "x", "y", "c"))
    every = ("z", "x", "y", "c")
    placed = (
        P(every, None),
        P(None, ("y", "c")),
        P(None, every, None),
        P(None, ("z", "x"), ("y", "c")),
        P(),
        P(),
    )
    return jax.shard_map(
        on_device,
        mesh=axes,
        in_specs=placed,
        out_specs=P(("z", "x"), ("y", "c")),
        check_vma=False,
    )
```

```python
import functools

import jax
import jax.numpy as jnp
from jax import lax
from jax.experimental import pallas as pl
from jax.experimental.pallas import tpu as pltpu
from jax.sharding import Mesh
from jax.sharding import PartitionSpec as P

NZ, NX, NY, NC = 8, 4, 4, 2
NDP = NZ * NX
SEG = 128
K = 8192
RANK = 64
COLS = 256
KQ = K // NY
BF16, F32 = jnp.bfloat16, jnp.float32
VMEM_LIMIT = 20 * 1024 * 1024
PACK = 8
STEP = 2048
AHEAD = 10**11


def params(**kw):
    return pltpu.CompilerParams(vmem_limit_bytes=VMEM_LIMIT, **kw)


def cost(flops, nbytes):
    return pl.CostEstimate(flops=flops, bytes_accessed=nbytes, transcendentals=0)


def in_hbm(x):
    return pltpu.with_memory_space_constraint(x, pltpu.HBM)


def shift(x, axis, by):
    n = {"y": NY, "c": NC}[axis]
    return lax.ppermute(x, axis, [(i, (i + by) % n) for i in range(n)])


def around(x, to_same_core=True):
    pairs = []
    for y in range(NY):
        for c in range(NC):
            to = (y + 1 - 2 * c) % NY
            pairs.append((y * NC + c, to * NC + (c if to_same_core else 1 - c)))
    return lax.ppermute(x, ("y", "c"), pairs)


def pack_kernel(apr, rps, down_ref, up_ref, out_ref, table, held, sems):
    def fill(a, carry):
        v = up_ref[a].astype(F32)
        table[a] = jnp.concatenate([v[:, :128], v[:, 128:]] * 2, axis=0)
        return carry

    lax.fori_loop(0, 64, fill, 0, unroll=8)
    row = lax.broadcasted_iota(jnp.int32, (8, 128), 0)

    def copy(g):
        part = pl.ds(PACK * g, PACK)
        return pltpu.make_async_copy(held.at[part], out_ref.at[part], sems.at[g])

    for g in range(NDP * NC // PACK):

        def to_device(n, carry):
            first = n // NC * (NY * NC) + n % NC
            ids = [apr[rps[first + s * NC]] for s in range(NY)]
            for s in range(NY):
                held[n, 32 * s : 32 * s + 32, :] = down_ref[ids[s]]
            ups = [
                jnp.where(row < 4, table[ids[s]], table[ids[s + 1]]) for s in (0, 2)
            ]
            held[n, 128:144, :] = jnp.concatenate(ups, axis=0).astype(BF16)
            return carry

        lax.fori_loop(PACK * g, PACK * g + PACK, to_device, 0, unroll=8)
        copy(g).start()
    for g in range(NDP * NC // PACK):
        copy(g).wait()


def pack(apr, rps, down, up):
    return pl.pallas_call(
        pack_kernel,
        grid_spec=pltpu.PrefetchScalarGridSpec(
            num_scalar_prefetch=2,
            grid=(1,),
            in_specs=[
                pl.BlockSpec((64, 32, 128), lambda i, *_: (0, 0, 0)),
                pl.BlockSpec((64, 2, COLS), lambda i, *_: (0, 0, 0)),
            ],
            out_specs=pl.BlockSpec(memory_space=pl.ANY),
            scratch_shapes=[
                pltpu.VMEM((64, 8, 128), F32),
                pltpu.VMEM((NDP * NC, 144, 128), BF16),
                pltpu.SemaphoreType.DMA((NDP * NC // PACK,)),
            ],
        ),
        out_shape=jax.ShapeDtypeStruct((NDP * NC, 144, 128), BF16),
        compiler_params=pltpu.CompilerParams(vmem_limit_bytes=60 * 1024 * 1024),
        cost_estimate=cost(0, 3 << 20),
    )(apr, rps, down, up)


def quarter_of(x_ref, q, pair):
    at = pair * 512 + (q // 2) * 128
    a = x_ref[:, pl.ds(pl.multiple_of(at, 128), 128)]
    b = x_ref[:, pl.ds(pl.multiple_of(at + 256, 128), 128)]
    low = jnp.concatenate([a[:, :64], b[:, :64]], axis=1)
    high = jnp.concatenate([a[:, 64:], b[:, 64:]], axis=1)
    return jnp.where(q % 2 == 0, low, high)


def split_kernel(first, x_ref, *outs):
    for pair in range(16):
        lanes = slice(128 * pair, 128 * pair + 128)
        for i in range(NY):
            outs[i][:, lanes] = quarter_of(x_ref, (first[0] + i) % NY, pair)


def split_quarters(first, x):
    return pl.pallas_call(
        split_kernel,
        grid_spec=pltpu.PrefetchScalarGridSpec(
            num_scalar_prefetch=1,
            grid=(1,),
            in_specs=[pl.BlockSpec((SEG, K), lambda i, *_: (0, 0))],
            out_specs=[pl.BlockSpec((SEG, KQ), lambda i, *_: (0, 0))] * NY,
        ),
        out_shape=[jax.ShapeDtypeStruct((SEG, KQ), BF16)] * NY,
        compiler_params=params(),
        cost_estimate=cost(AHEAD, 4 * SEG * K),
    )(first, x)


def low_kernel(yc, x_ref, down_ref, after, *rest):
    outs, sums = rest[:NY], rest[NY]
    me, core = yc[0], yc[1]
    for i, d in enumerate((0, 3 - 2 * core, 1 + 2 * core, 2)):
        s = (me + d) & 3
        factor = down_ref[:, pl.ds(pl.multiple_of(32 * s, 32), 32), :].reshape(KQ, 128)
        sums[s] = jnp.dot(x_ref[i], factor, preferred_element_type=F32)
    lane = lax.broadcasted_iota(jnp.int32, (128, 128), 1)
    for e in range(NY):
        value = ((me + e) & 3) >= 2
        for pair in range(2):
            a, b = sums[2 * pair], sums[2 * pair + 1]
            keys = jnp.where(lane < 64, a, pltpu.roll(b, 64, 1))
            values = jnp.where(lane < 64, pltpu.roll(a, 64, 1), b)
            outs[e][128 * pair : 128 * pair + 128, :] = jnp.where(value, values, keys)


def low_parts(yc, x, recv, after):
    return pl.pallas_call(
        low_kernel,
        grid_spec=pltpu.PrefetchScalarGridSpec(
            num_scalar_prefetch=1,
            grid=(1,),
            in_specs=[
                pl.BlockSpec((4, SEG, KQ), lambda i, *_: (0, 0, 0)),
                pl.BlockSpec((64, 128, 128), lambda i, *_: (0, 0, 0)),
                pl.BlockSpec(memory_space=pl.ANY),
            ],
            out_specs=[pl.BlockSpec((256, 128), lambda i, *_: (0, 0))] * NY,
            scratch_shapes=[pltpu.VMEM((NY, 128, 128), F32)],
        ),
        out_shape=[jax.ShapeDtypeStruct((256, 128), F32)] * NY,
        compiler_params=params(),
        cost_estimate=cost(2 * 512 * KQ * 128, 5 << 20),
    )(yc, x, recv, after)


def up_kernel(recv_ref, out_ref):
    r = lax.broadcasted_iota(jnp.int32, (512, 512), 0)
    k = lax.broadcasted_iota(jnp.int32, (512, 512), 1)
    pair, half, seg, rank = r // 256, (r // 128) % 2, (r // 64) % 2, r % 64
    source = (rank // 2) * 16 + (pair * 2 + seg) * 4 + half * 2 + rank % 2
    order = (k == source).astype(F32).astype(BF16)
    every = recv_ref[...].reshape(NDP, NC, 16, 128)
    for c in range(NC):
        rows = every[:, c].reshape(512, 128)
        got = jnp.dot(order, rows, preferred_element_type=F32).astype(BF16)
        for p in range(2):
            for h in range(2):
                at = 256 * p + 128 * h
                out_ref[c, p, :, 128 * h : 128 * h + 128] = got[at : at + 128]


def up_rows(recv):
    return pl.pallas_call(
        up_kernel,
        grid=(1,),
        in_specs=[pl.BlockSpec((64, 16, 128), lambda i: (0, 8, 0))],
        out_specs=pl.BlockSpec((NC, 2, 128, COLS), lambda i: (0, 0, 0, 0)),
        out_shape=jax.ShapeDtypeStruct((NC, 2, 128, COLS), BF16),
        compiler_params=params(),
        cost_estimate=cost(2 * 512 * 512 * 256, 1 << 19),
    )(recv)


def near_kernel(n, yc, *refs):
    xs, (w0, w1) = refs[:n], refs[n : n + 2]
    out, quarters = refs[-n - 1], refs[-n:]

    @pl.when(pl.program_id(0) == 0)
    def _():
        out[...] = jnp.zeros_like(out)

    for x, quarter in zip(xs, quarters):
        for pair in range(STEP // 512):
            quarter[:, 128 * pair : 128 * pair + 128] = quarter_of(x, yc[0], pair)
    x = jnp.concatenate([x[...] for x in xs], axis=0)
    out[:, :COLS] += jnp.dot(x, w0[...], preferred_element_type=F32)
    out[:, COLS:] += jnp.dot(x, w1[...], preferred_element_type=F32)


def near_base(yc, xs, w0, w1, after=()):
    step, n = STEP, len(xs)
    weight = pl.BlockSpec((step, COLS), lambda i, yc: (i, 0))
    result = pl.pallas_call(
        functools.partial(near_kernel, n),
        grid_spec=pltpu.PrefetchScalarGridSpec(
            num_scalar_prefetch=1,
            grid=(K // step,),
            in_specs=[pl.BlockSpec((SEG, step), lambda i, yc: (0, i))] * n
            + [weight] * 2
            + [pl.BlockSpec(memory_space=pl.ANY)] * len(after),
            out_specs=[pl.BlockSpec((SEG * n, 2 * COLS), lambda i, yc: (0, 0))]
            + [pl.BlockSpec((SEG, step // NY), lambda i, yc: (0, i))] * n,
        ),
        out_shape=[jax.ShapeDtypeStruct((SEG * n, 2 * COLS), F32)]
        + [jax.ShapeDtypeStruct((SEG, KQ), BF16)] * n,
        compiler_params=params(),
        cost_estimate=cost(2 * SEG * n * K * 512, 12 << 20),
    )(yc, *xs, w0, w1, *after)
    return result[0], result[1:]


def quarter_weight(offset):
    return pl.BlockSpec((32, None, 64, COLS), lambda i, yc: (0, (yc[0] + offset(i)) % NY, 0, 0))


def far_kernel(yc, q0, q1, w0, w1, own, near, other, out, stack):
    i = pl.program_id(0)

    @pl.when(i == 0)
    def _():
        out[...] = jnp.zeros_like(out)
        for j, x in enumerate((own, near, other, q0)):
            stack[j] = x[...]

    x = jnp.where(i == 0, q0[...], q1[...])
    out[:, :COLS] += jnp.dot(x, w0[...].reshape(KQ, COLS), preferred_element_type=F32)
    out[:, COLS:] += jnp.dot(x, w1[...].reshape(KQ, COLS), preferred_element_type=F32)


def far_base(yc, q0, q1, w0, w1, quarters):
    weight = quarter_weight(lambda i: i)
    return pl.pallas_call(
        far_kernel,
        grid_spec=pltpu.PrefetchScalarGridSpec(
            num_scalar_prefetch=1,
            grid=(2,),
            in_specs=[whole(SEG, KQ)] * 2 + [weight] * 2 + [whole(SEG, KQ)] * 3,
            out_specs=[whole(SEG, 512), whole(4, SEG, KQ)],
        ),
        out_shape=[
            jax.ShapeDtypeStruct((SEG, 512), F32),
            jax.ShapeDtypeStruct((4, SEG, KQ), BF16),
        ],
        compiler_params=params(),
        cost_estimate=cost(2 * SEG * 2 * KQ * 512, 10 << 20),
    )(yc, q0, q1, w0, w1, *quarters)


def more_kernel(yc, x, w0, w1, before, out):
    x = x[...]
    out[:, :COLS] = before[:, :COLS] + jnp.dot(
        x, w0[...].reshape(KQ, COLS), preferred_element_type=F32
    )
    out[:, COLS:] = before[:, COLS:] + jnp.dot(
        x, w1[...].reshape(KQ, COLS), preferred_element_type=F32
    )


def more_base(yc, x, quarter, w0, w1, before):
    weight = quarter_weight(lambda i: quarter)
    return pl.pallas_call(
        more_kernel,
        grid_spec=pltpu.PrefetchScalarGridSpec(
            num_scalar_prefetch=1,
            grid=(1,),
            in_specs=[whole(SEG, KQ), weight, weight, whole(SEG, 512)],
            out_specs=whole(SEG, 512),
        ),
        out_shape=jax.ShapeDtypeStruct((SEG, 512), F32),
        compiler_params=params(),
        cost_estimate=cost(2 * SEG * KQ * 512, 3 << 20),
    )(yc, x, w0, w1, before)


def whole(*shape):
    return pl.BlockSpec(shape, lambda i, yc: (0,) * len(shape))


def sum_kernel(yc, first, second, far, p0, p1, p2, p3, up, out, out_partner):
    me, core = yc[0], yc[1]
    low = (p0[...] + p1[...] + p2[...] + p3[...]).astype(BF16).astype(F32)
    left = lax.broadcasted_iota(jnp.int32, (128, 128), 1) < 64
    bases = (first[:SEG, :], first[SEG:, :], second[...], far[...])
    for d, base in zip((0, 3 - 2 * core, 1 + 2 * core, 2), bases):
        s = (me + d) & 3
        both = jnp.where(s < 2, low[:SEG], low[SEG:])
        mine = jnp.where(left == (s & 1 == 0), both, 0.0).astype(BF16)
        own = jnp.dot(mine, up[core, s // 2], preferred_element_type=F32)
        other = jnp.dot(mine, up[1 - core, s // 2], preferred_element_type=F32)
        out[s] = (base[:, :COLS] + own).astype(BF16)
        out_partner[s] = (base[:, COLS:] + other).astype(BF16)


def sum_up(yc, first, second, far, parts, up):
    return pl.pallas_call(
        sum_kernel,
        grid_spec=pltpu.PrefetchScalarGridSpec(
            num_scalar_prefetch=1,
            grid=(1,),
            in_specs=[whole(2 * SEG, 512), whole(SEG, 512), whole(SEG, 512)]
            + [whole(256, 128)] * NY
            + [whole(NC, 2, 128, COLS)],
            out_specs=[
                pl.BlockSpec((NY, None, SEG, COLS), lambda i, yc: (0, yc[1], 0, 0)),
                whole(NY, SEG, COLS),
            ],
        ),
        out_shape=[
            jax.ShapeDtypeStruct((NY, NC, SEG, COLS), BF16),
            jax.ShapeDtypeStruct((NY, SEG, COLS), BF16),
        ],
        compiler_params=params(),
        cost_estimate=cost(2 * 512 * 128 * 512, 3 << 20),
    )(yc, first, second, far, *parts, up)


def on_device(tokens, weight, down, up, apr, rps):
    y, c = lax.axis_index("y"), lax.axis_index("c")
    yc = jnp.stack([y, c]).astype(jnp.int32)

    near = around(tokens)
    partner_tokens = shift(tokens, "c", 1)
    other = around(partner_tokens, False)
    ahead = ((y + 1 - 2 * c + NY) & 3).reshape(1).astype(jnp.int32)
    q0, q1, q2, q3 = [around(v) for v in split_quarters(ahead, near)]

    send = pack(apr, rps, down, up)
    recv = lax.all_to_all(send, ("z", "x", "c"), 0, 0)
    partner_weight = shift(weight, "c", 1)

    w0 = weight.reshape(32, NY, 64, COLS)
    w1 = partner_weight.reshape(32, NY, 64, COLS)
    first, quarters = near_base(yc, [tokens, near], weight, partner_weight)
    second, more = near_base(yc, [other], weight, partner_weight, (first,))
    far, stack = far_base(yc, q0, q1, w0, w1, [*quarters, *more])
    far = more_base(yc, q2, 2, w0, w1, far)

    parts = low_parts(yc, stack, recv, far)
    far = more_base(yc, q3, 3, w0, w1, far)
    parts = [parts[0]] + [shift(parts[e], "y", e) for e in (2, 1, 3)]
    up_sorted = up_rows(recv)
    out, out_partner = sum_up(yc, first, second, far, parts, up_sorted)
    theirs = shift(out_partner, "c", 1)
    zero = jnp.zeros((), jnp.int32)
    out = lax.dynamic_update_slice(
        out, theirs[:, None], (zero, (1 - c).astype(jnp.int32), zero, zero)
    )
    return out.reshape(NY * NC * SEG, COLS)


def solution(mesh):
    axes = Mesh(mesh.devices.reshape(NZ, NX, NY, NC), ("z", "x", "y", "c"))
    every = ("z", "x", "y", "c")
    placed = (
        P(every, None),
        P(None, ("y", "c")),
        P(None, every, None),
        P(None, ("z", "x"), ("y", "c")),
        P(),
        P(),
    )
    return jax.shard_map(
        on_device,
        mesh=axes,
        in_specs=placed,
        out_specs=P(("z", "x"), ("y", "c")),
        check_vma=False,
    )
```

```python
import functools

import jax
import jax.numpy as jnp
from jax import lax
from jax.experimental import pallas as pl
from jax.experimental.pallas import tpu as pltpu
from jax.sharding import Mesh
from jax.sharding import PartitionSpec as P

NZ, NX, NY, NC = 8, 4, 4, 2
NDP = NZ * NX
SEG = 128
K = 8192
RANK = 64
COLS = 256
KQ = K // NY
BF16, F32 = jnp.bfloat16, jnp.float32
VMEM_LIMIT = 20 * 1024 * 1024
PACK = 8
STEP = 2048
AHEAD = 10**11


def params(**kw):
    return pltpu.CompilerParams(vmem_limit_bytes=VMEM_LIMIT, **kw)


def cost(flops, nbytes):
    return pl.CostEstimate(flops=flops, bytes_accessed=nbytes, transcendentals=0)


def in_hbm(x):
    return pltpu.with_memory_space_constraint(x, pltpu.HBM)


def shift(x, axis, by):
    n = {"y": NY, "c": NC}[axis]
    return lax.ppermute(x, axis, [(i, (i + by) % n) for i in range(n)])


def around(x, to_same_core=True):
    pairs = []
    for y in range(NY):
        for c in range(NC):
            to = (y + 1 - 2 * c) % NY
            pairs.append((y * NC + c, to * NC + (c if to_same_core else 1 - c)))
    return lax.ppermute(x, ("y", "c"), pairs)


def pack_kernel(apr, rps, down_ref, up_ref, out_ref, table, held, sems):
    def fill(a, carry):
        v = up_ref[a].astype(F32)
        table[a] = jnp.concatenate([v[:, :128], v[:, 128:]] * 2, axis=0)
        return carry

    lax.fori_loop(0, 64, fill, 0, unroll=8)
    row = lax.broadcasted_iota(jnp.int32, (8, 128), 0)

    def copy(g):
        part = pl.ds(PACK * g, PACK)
        return pltpu.make_async_copy(held.at[part], out_ref.at[part], sems.at[g])

    for g in range(NDP * NC // PACK):

        def to_device(n, carry):
            first = n // NC * (NY * NC) + n % NC
            ids = [apr[rps[first + s * NC]] for s in range(NY)]
            for s in range(NY):
                held[n, 32 * s : 32 * s + 32, :] = down_ref[ids[s]]
            ups = [
                jnp.where(row < 4, table[ids[s]], table[ids[s + 1]]) for s in (0, 2)
            ]
            held[n, 128:144, :] = jnp.concatenate(ups, axis=0).astype(BF16)
            return carry

        lax.fori_loop(PACK * g, PACK * g + PACK, to_device, 0, unroll=8)
        copy(g).start()
    for g in range(NDP * NC // PACK):
        copy(g).wait()


def pack(apr, rps, down, up):
    return pl.pallas_call(
        pack_kernel,
        in_specs=[
            pl.BlockSpec(memory_space=pltpu.SMEM),
            pl.BlockSpec(memory_space=pltpu.SMEM),
            pl.BlockSpec(memory_space=pltpu.VMEM),
            pl.BlockSpec(memory_space=pltpu.VMEM),
        ],
        out_specs=pl.BlockSpec(memory_space=pl.ANY),
        scratch_shapes=[
            pltpu.VMEM((64, 8, 128), F32),
            pltpu.VMEM((NDP * NC, 144, 128), BF16),
            pltpu.SemaphoreType.DMA((NDP * NC // PACK,)),
        ],
        out_shape=jax.ShapeDtypeStruct((NDP * NC, 144, 128), BF16),
        compiler_params=pltpu.CompilerParams(vmem_limit_bytes=60 * 1024 * 1024),
        cost_estimate=cost(0, 3 << 20),
    )(apr, rps, down, up)


def quarter_of(x_ref, q, pair):
    at = pair * 512 + (q // 2) * 128
    a = x_ref[:, pl.ds(pl.multiple_of(at, 128), 128)]
    b = x_ref[:, pl.ds(pl.multiple_of(at + 256, 128), 128)]
    low = jnp.concatenate([a[:, :64], b[:, :64]], axis=1)
    high = jnp.concatenate([a[:, 64:], b[:, 64:]], axis=1)
    return jnp.where(q % 2 == 0, low, high)


def split_kernel(first, x_ref, *outs):
    for pair in range(16):
        lanes = slice(128 * pair, 128 * pair + 128)
        for i in range(NY):
            outs[i][:, lanes] = quarter_of(x_ref, (first[0] + i) % NY, pair)


def split_quarters(first, x):
    return pl.pallas_call(
        split_kernel,
        grid_spec=pltpu.PrefetchScalarGridSpec(
            num_scalar_prefetch=1,
            grid=(1,),
            in_specs=[pl.BlockSpec((SEG, K), lambda i, *_: (0, 0))],
            out_specs=[pl.BlockSpec((SEG, KQ), lambda i, *_: (0, 0))] * NY,
        ),
        out_shape=[jax.ShapeDtypeStruct((SEG, KQ), BF16)] * NY,
        compiler_params=params(),
        cost_estimate=cost(AHEAD, 4 * SEG * K),
    )(first, x)


def low_kernel(yc, x_ref, recv_ref, after, *rest):
    outs, sums = rest[:NY], rest[NY]
    me, core = yc[0], yc[1]
    for i, d in enumerate((0, 3 - 2 * core, 1 + 2 * core, 2)):
        s = (me + d) & 3
        factor = recv_ref[:, pl.ds(pl.multiple_of(32 * s, 32), 32), :].reshape(KQ, 128)
        sums[s] = jnp.dot(x_ref[i], factor, preferred_element_type=F32)
    lane = lax.broadcasted_iota(jnp.int32, (128, 128), 1)
    for e in range(NY):
        value = (me + e) % NY >= NY // 2
        for pair in range(2):
            a, b = sums[2 * pair], sums[2 * pair + 1]
            keys = jnp.where(lane < 64, a, pltpu.roll(b, 64, 1))
            values = jnp.where(lane < 64, pltpu.roll(a, 64, 1), b)
            outs[e][128 * pair : 128 * pair + 128, :] = jnp.where(value, values, keys)


SMEM = pl.BlockSpec(memory_space=pltpu.SMEM)
VMEM = pl.BlockSpec(memory_space=pltpu.VMEM)
ANY = pl.BlockSpec(memory_space=pl.ANY)


def low_parts(yc, x, recv, after):
    return pl.pallas_call(
        low_kernel,
        in_specs=[SMEM, VMEM, VMEM, ANY],
        out_specs=[VMEM] * NY,
        scratch_shapes=[pltpu.VMEM((NY, 128, 128), F32)],
        out_shape=[jax.ShapeDtypeStruct((256, 128), F32)] * NY,
        compiler_params=params(),
        cost_estimate=cost(2 * 512 * KQ * 128, 5 << 20),
    )(yc, x, recv, after)


def up_kernel(recv_ref, out_ref):
    r = lax.broadcasted_iota(jnp.int32, (512, 512), 0)
    k = lax.broadcasted_iota(jnp.int32, (512, 512), 1)
    pair, half, seg, rank = r // 256, (r // 128) % 2, (r // 64) % 2, r % 64
    source = (rank // 2) * 16 + (pair * 2 + seg) * 4 + half * 2 + rank % 2
    order = (k == source).astype(F32).astype(BF16)
    every = recv_ref[:, 128:, :].reshape(NDP, NC, 16, 128)
    for c in range(NC):
        rows = every[:, c].reshape(512, 128)
        got = jnp.dot(order, rows, preferred_element_type=F32).astype(BF16)
        for p in range(2):
            for h in range(2):
                at = 256 * p + 128 * h
                out_ref[c, p, :, 128 * h : 128 * h + 128] = got[at : at + 128]


def up_rows(recv):
    return pl.pallas_call(
        up_kernel,
        in_specs=[VMEM],
        out_specs=VMEM,
        out_shape=jax.ShapeDtypeStruct((NC, 2, 128, COLS), BF16),
        compiler_params=params(),
        cost_estimate=cost(2 * 512 * 512 * 256, 1 << 19),
    )(recv)


def near_kernel(n, yc, *refs):
    xs, (w0, w1) = refs[:n], refs[n : n + 2]
    out, quarters = refs[-n - 1], refs[-n:]

    @pl.when(pl.program_id(0) == 0)
    def _():
        out[...] = jnp.zeros_like(out)

    for x, quarter in zip(xs, quarters):
        for pair in range(STEP // 512):
            quarter[:, 128 * pair : 128 * pair + 128] = quarter_of(x, yc[0], pair)
    x = jnp.concatenate([x[...] for x in xs], axis=0)
    out[:, :COLS] += jnp.dot(x, w0[...], preferred_element_type=F32)
    out[:, COLS:] += jnp.dot(x, w1[...], preferred_element_type=F32)


def near_base(yc, xs, w0, w1, after=()):
    step, n = STEP, len(xs)
    weight = pl.BlockSpec((step, COLS), lambda i, yc: (i, 0))
    result = pl.pallas_call(
        functools.partial(near_kernel, n),
        grid_spec=pltpu.PrefetchScalarGridSpec(
            num_scalar_prefetch=1,
            grid=(K // step,),
            in_specs=[pl.BlockSpec((SEG, step), lambda i, yc: (0, i))] * n
            + [weight] * 2
            + [pl.BlockSpec(memory_space=pl.ANY)] * len(after),
            out_specs=[pl.BlockSpec((SEG * n, 2 * COLS), lambda i, yc: (0, 0))]
            + [pl.BlockSpec((SEG, step // NY), lambda i, yc: (0, i))] * n,
        ),
        out_shape=[jax.ShapeDtypeStruct((SEG * n, 2 * COLS), F32)]
        + [jax.ShapeDtypeStruct((SEG, KQ), BF16)] * n,
        compiler_params=params(),
        cost_estimate=cost(2 * SEG * n * K * 512, 12 << 20),
    )(yc, *xs, w0, w1, *after)
    return result[0], result[1:]


def quarter_weight(offset):
    return pl.BlockSpec((32, None, 64, COLS), lambda i, yc: (0, (yc[0] + offset(i)) % NY, 0, 0))


def far_kernel(yc, q0, q1, w0, w1, own, near, other, out, stack):
    i = pl.program_id(0)

    @pl.when(i == 0)
    def _():
        out[...] = jnp.zeros_like(out)
        for j, x in enumerate((own, near, other, q0)):
            stack[j] = x[...]

    x = jnp.where(i == 0, q0[...], q1[...])
    out[:, :COLS] += jnp.dot(x, w0[...].reshape(KQ, COLS), preferred_element_type=F32)
    out[:, COLS:] += jnp.dot(x, w1[...].reshape(KQ, COLS), preferred_element_type=F32)


def far_base(yc, q0, q1, w0, w1, quarters):
    weight = quarter_weight(lambda i: i)
    return pl.pallas_call(
        far_kernel,
        grid_spec=pltpu.PrefetchScalarGridSpec(
            num_scalar_prefetch=1,
            grid=(2,),
            in_specs=[whole(SEG, KQ)] * 2 + [weight] * 2 + [whole(SEG, KQ)] * 3,
            out_specs=[whole(SEG, 512), whole(4, SEG, KQ)],
        ),
        out_shape=[
            jax.ShapeDtypeStruct((SEG, 512), F32),
            jax.ShapeDtypeStruct((4, SEG, KQ), BF16),
        ],
        compiler_params=params(),
        cost_estimate=cost(2 * SEG * 2 * KQ * 512, 10 << 20),
    )(yc, q0, q1, w0, w1, *quarters)


def more_kernel(yc, x, w0, w1, before, out):
    x = x[...]
    out[:, :COLS] = before[:, :COLS] + jnp.dot(
        x, w0[...].reshape(KQ, COLS), preferred_element_type=F32
    )
    out[:, COLS:] = before[:, COLS:] + jnp.dot(
        x, w1[...].reshape(KQ, COLS), preferred_element_type=F32
    )


def more_base(yc, x, quarter, w0, w1, before):
    weight = quarter_weight(lambda i: quarter)
    return pl.pallas_call(
        more_kernel,
        grid_spec=pltpu.PrefetchScalarGridSpec(
            num_scalar_prefetch=1,
            grid=(1,),
            in_specs=[whole(SEG, KQ), weight, weight, whole(SEG, 512)],
            out_specs=whole(SEG, 512),
        ),
        out_shape=jax.ShapeDtypeStruct((SEG, 512), F32),
        compiler_params=params(),
        cost_estimate=cost(2 * SEG * KQ * 512, 3 << 20),
    )(yc, x, w0, w1, before)


def whole(*shape):
    return pl.BlockSpec(shape, lambda i, yc: (0,) * len(shape))


def sum_kernel(
    yc, first, second, far, p0, p1, p2, p3, up, out, out_partner, held, sem
):
    me, core = yc[0], yc[1]
    low = (p0[...] + p1[...] + p2[...] + p3[...]).astype(BF16).astype(F32)
    left = lax.broadcasted_iota(jnp.int32, (128, 128), 1) < 64
    bases = (first[:SEG, :], first[SEG:, :], second[...], far[...])
    for d, base in zip((0, 3 - 2 * core, 1 + 2 * core, 2), bases):
        s = (me + d) & 3
        both = jnp.where(s < 2, low[:SEG], low[SEG:])
        mine = jnp.where(left == (s & 1 == 0), both, 0.0).astype(BF16)
        own = jnp.dot(mine, up[core, s // 2], preferred_element_type=F32)
        other = jnp.dot(mine, up[1 - core, s // 2], preferred_element_type=F32)
        held[s] = (base[:, :COLS] + own).astype(BF16)
        out_partner[s] = (base[:, COLS:] + other).astype(BF16)
    copy = pltpu.make_async_copy(held, out.at[:, core], sem)
    copy.start()
    copy.wait()


def sum_up(yc, first, second, far, parts, up):
    return pl.pallas_call(
        sum_kernel,
        in_specs=[SMEM] + [VMEM] * 8,
        out_specs=[ANY, VMEM],
        out_shape=[
            jax.ShapeDtypeStruct((NY, NC, SEG, COLS), BF16),
            jax.ShapeDtypeStruct((NY, SEG, COLS), BF16),
        ],
        scratch_shapes=[
            pltpu.VMEM((NY, SEG, COLS), BF16),
            pltpu.SemaphoreType.DMA(()),
        ],
        compiler_params=params(),
        cost_estimate=cost(2 * 512 * 128 * 512, 3 << 20),
    )(yc, first, second, far, *parts, up)


def on_device(tokens, weight, down, up, apr, rps):
    y, c = lax.axis_index("y"), lax.axis_index("c")
    yc = jnp.stack([y, c]).astype(jnp.int32)

    send = pack(apr, rps, down, up)
    tokens, send = lax.optimization_barrier((tokens, send))
    near = around(tokens)
    partner_tokens = shift(tokens, "c", 1)
    other = around(partner_tokens, False)
    ahead = ((y + 1 - 2 * c + NY) & 3).reshape(1).astype(jnp.int32)
    q0, q1, q2, q3 = [around(v) for v in split_quarters(ahead, near)]

    recv = lax.all_to_all(send, ("z", "x", "c"), 0, 0)
    weight, _ = lax.optimization_barrier((weight, partner_tokens))
    partner_weight = shift(weight, "c", 1)

    w0 = weight.reshape(32, NY, 64, COLS)
    w1 = partner_weight.reshape(32, NY, 64, COLS)
    first, quarters = near_base(yc, [tokens, near], weight, partner_weight)
    second, more = near_base(yc, [other], weight, partner_weight, (first,))
    far, stack = far_base(yc, q0, q1, w0, w1, [*quarters, *more])

    far = more_base(yc, q2, 2, w0, w1, far)
    parts = low_parts(yc, stack, recv, far)
    far = more_base(yc, q3, 3, in_hbm(w0), in_hbm(w1), far)
    parts = [parts[0]] + [shift(parts[e], "y", e) for e in (1, 2, 3)]
    up_sorted = up_rows(recv)
    out, out_partner = sum_up(yc, first, second, far, parts, up_sorted)
    theirs = shift(out_partner, "c", 1)
    zero = jnp.zeros((), jnp.int32)
    out = lax.dynamic_update_slice(
        out, theirs[:, None], (zero, (1 - c).astype(jnp.int32), zero, zero)
    )
    return out.reshape(NY * NC * SEG, COLS)


def solution(mesh):
    axes = Mesh(mesh.devices.reshape(NZ, NX, NY, NC), ("z", "x", "y", "c"))
    every = ("z", "x", "y", "c")
    placed = (
        P(every, None),
        P(None, ("y", "c")),
        P(None, every, None),
        P(None, ("z", "x"), ("y", "c")),
        P(),
        P(),
    )
    return jax.shard_map(
        on_device,
        mesh=axes,
        in_specs=placed,
        out_specs=P(("z", "x"), ("y", "c")),
        check_vma=False,
    )
```

```python
import functools

import jax
import jax.numpy as jnp
from jax import lax
from jax.experimental import pallas as pl
from jax.experimental.pallas import tpu as pltpu
from jax.sharding import Mesh
from jax.sharding import PartitionSpec as P

NZ, NX, NY, NC = 8, 4, 4, 2
NDP = NZ * NX
SEG = 128
K = 8192
RANK = 64
COLS = 256
KQ = K // NY
BF16, F32 = jnp.bfloat16, jnp.float32
VMEM_LIMIT = 20 * 1024 * 1024
PACK = 8
STEP = 2048
AHEAD = 10**11


def params(**kw):
    return pltpu.CompilerParams(vmem_limit_bytes=VMEM_LIMIT, **kw)


def cost(flops, nbytes):
    return pl.CostEstimate(flops=flops, bytes_accessed=nbytes, transcendentals=0)


def in_hbm(x):
    return pltpu.with_memory_space_constraint(x, pltpu.HBM)


def shift(x, axis, by):
    n = {"y": NY, "c": NC}[axis]
    return lax.ppermute(x, axis, [(i, (i + by) % n) for i in range(n)])


def around(x, to_same_core=True):
    pairs = []
    for y in range(NY):
        for c in range(NC):
            to = (y + 1 - 2 * c) % NY
            pairs.append((y * NC + c, to * NC + (c if to_same_core else 1 - c)))
    return lax.ppermute(x, ("y", "c"), pairs)


def pack_kernel(apr, rps, down_ref, up_ref, out_ref, table, held, sems):
    def fill(a, carry):
        v = up_ref[a].astype(F32)
        table[a] = jnp.concatenate([v[:, :128], v[:, 128:]] * 2, axis=0)
        return carry

    lax.fori_loop(0, 64, fill, 0, unroll=8)
    row = lax.broadcasted_iota(jnp.int32, (8, 128), 0)

    def copy(g):
        part = pl.ds(PACK * g, PACK)
        return pltpu.make_async_copy(held.at[part], out_ref.at[part], sems.at[g])

    for g in range(NDP * NC // PACK):

        def to_device(n, carry):
            first = n // NC * (NY * NC) + n % NC
            ids = [apr[rps[first + s * NC]] for s in range(NY)]
            for s in range(NY):
                held[n, 32 * s : 32 * s + 32, :] = down_ref[ids[s]]
            ups = [
                jnp.where(row < 4, table[ids[s]], table[ids[s + 1]]) for s in (0, 2)
            ]
            held[n, 128:144, :] = jnp.concatenate(ups, axis=0).astype(BF16)
            return carry

        lax.fori_loop(PACK * g, PACK * g + PACK, to_device, 0, unroll=8)
        copy(g).start()
    for g in range(NDP * NC // PACK):
        copy(g).wait()


def pack(apr, rps, down, up):
    return pl.pallas_call(
        pack_kernel,
        in_specs=[
            pl.BlockSpec(memory_space=pltpu.SMEM),
            pl.BlockSpec(memory_space=pltpu.SMEM),
            pl.BlockSpec(memory_space=pltpu.VMEM),
            pl.BlockSpec(memory_space=pltpu.VMEM),
        ],
        out_specs=pl.BlockSpec(memory_space=pl.ANY),
        scratch_shapes=[
            pltpu.VMEM((64, 8, 128), F32),
            pltpu.VMEM((NDP * NC, 144, 128), BF16),
            pltpu.SemaphoreType.DMA((NDP * NC // PACK,)),
        ],
        out_shape=jax.ShapeDtypeStruct((NDP * NC, 144, 128), BF16),
        compiler_params=pltpu.CompilerParams(vmem_limit_bytes=60 * 1024 * 1024),
        cost_estimate=cost(0, 3 << 20),
    )(apr, rps, down, up)


def quarter_of(x_ref, q, pair):
    at = pair * 512 + (q // 2) * 128
    a = x_ref[:, pl.ds(pl.multiple_of(at, 128), 128)]
    b = x_ref[:, pl.ds(pl.multiple_of(at + 256, 128), 128)]
    low = jnp.concatenate([a[:, :64], b[:, :64]], axis=1)
    high = jnp.concatenate([a[:, 64:], b[:, 64:]], axis=1)
    return jnp.where(q % 2 == 0, low, high)


def split_kernel(first, x_ref, *outs):
    for pair in range(16):
        lanes = slice(128 * pair, 128 * pair + 128)
        for i in range(NY):
            outs[i][:, lanes] = quarter_of(x_ref, (first[0] + i) % NY, pair)


def split_quarters(first, x):
    return pl.pallas_call(
        split_kernel,
        grid_spec=pltpu.PrefetchScalarGridSpec(
            num_scalar_prefetch=1,
            grid=(1,),
            in_specs=[pl.BlockSpec((SEG, K), lambda i, *_: (0, 0))],
            out_specs=[pl.BlockSpec((SEG, KQ), lambda i, *_: (0, 0))] * NY,
        ),
        out_shape=[jax.ShapeDtypeStruct((SEG, KQ), BF16)] * NY,
        compiler_params=params(),
        cost_estimate=cost(AHEAD, 4 * SEG * K),
    )(first, x)


def low_kernel(yc, x_ref, recv_ref, after, *rest):
    outs, sums = rest[:NY], rest[NY]
    me, core = yc[0], yc[1]
    for i, d in enumerate((0, 3 - 2 * core, 1 + 2 * core, 2)):
        s = (me + d) & 3
        factor = recv_ref[:, pl.ds(pl.multiple_of(32 * s, 32), 32), :].reshape(KQ, 128)
        sums[s] = jnp.dot(x_ref[i], factor, preferred_element_type=F32)
    lane = lax.broadcasted_iota(jnp.int32, (128, 128), 1)
    for pair in range(2):
        rows = slice(128 * pair, 128 * pair + 128)
        a, b = sums[2 * pair], sums[2 * pair + 1]
        keys = jnp.where(lane < 64, a, pltpu.roll(b, 64, 1))
        values = jnp.where(lane < 64, pltpu.roll(a, 64, 1), b)
        for e in range(NY):
            outs[e][rows, :] = jnp.where(((me + e) & 3) >= 2, values, keys)


SMEM = pl.BlockSpec(memory_space=pltpu.SMEM)
VMEM = pl.BlockSpec(memory_space=pltpu.VMEM)
ANY = pl.BlockSpec(memory_space=pl.ANY)


def low_parts(yc, x, recv, after):
    return pl.pallas_call(
        low_kernel,
        in_specs=[SMEM, VMEM, VMEM, ANY],
        out_specs=[VMEM] * NY,
        scratch_shapes=[pltpu.VMEM((NY, 128, 128), F32)],
        out_shape=[jax.ShapeDtypeStruct((256, 128), F32)] * NY,
        compiler_params=params(),
        cost_estimate=cost(2 * 512 * KQ * 128, 5 << 20),
    )(yc, x, recv, after)


def up_kernel(recv_ref, out_ref):
    r = lax.broadcasted_iota(jnp.int32, (512, 512), 0)
    k = lax.broadcasted_iota(jnp.int32, (512, 512), 1)
    pair, half, seg, rank = r // 256, (r // 128) % 2, (r // 64) % 2, r % 64
    source = (rank // 2) * 16 + (pair * 2 + seg) * 4 + half * 2 + rank % 2
    order = (k == source).astype(F32).astype(BF16)
    every = recv_ref[:, 128:, :].reshape(NDP, NC, 16, 128)
    for c in range(NC):
        rows = every[:, c].reshape(512, 128)
        got = jnp.dot(order, rows, preferred_element_type=F32).astype(BF16)
        for p in range(2):
            for h in range(2):
                at = 256 * p + 128 * h
                out_ref[c, p, :, 128 * h : 128 * h + 128] = got[at : at + 128]


def up_rows(recv):
    return pl.pallas_call(
        up_kernel,
        in_specs=[VMEM],
        out_specs=VMEM,
        out_shape=jax.ShapeDtypeStruct((NC, 2, 128, COLS), BF16),
        compiler_params=params(),
        cost_estimate=cost(2 * 512 * 512 * 256, 1 << 19),
    )(recv)


def near_kernel(n, yc, *refs):
    xs, (w0, w1) = refs[:n], refs[n : n + 2]
    out, quarters = refs[-n - 1], refs[-n:]

    @pl.when(pl.program_id(0) == 0)
    def _():
        out[...] = jnp.zeros_like(out)

    for x, quarter in zip(xs, quarters):
        for pair in range(STEP // 512):
            quarter[:, 128 * pair : 128 * pair + 128] = quarter_of(x, yc[0], pair)
    x = jnp.concatenate([x[...] for x in xs], axis=0)
    out[:, :COLS] += jnp.dot(x, w0[...], preferred_element_type=F32)
    out[:, COLS:] += jnp.dot(x, w1[...], preferred_element_type=F32)


def near_base(yc, xs, w0, w1, after=()):
    step, n = STEP, len(xs)
    weight = pl.BlockSpec((step, COLS), lambda i, yc: (i, 0))
    result = pl.pallas_call(
        functools.partial(near_kernel, n),
        grid_spec=pltpu.PrefetchScalarGridSpec(
            num_scalar_prefetch=1,
            grid=(K // step,),
            in_specs=[pl.BlockSpec((SEG, step), lambda i, yc: (0, i))] * n
            + [weight] * 2
            + [pl.BlockSpec(memory_space=pl.ANY)] * len(after),
            out_specs=[pl.BlockSpec((SEG * n, 2 * COLS), lambda i, yc: (0, 0))]
            + [pl.BlockSpec((SEG, step // NY), lambda i, yc: (0, i))] * n,
        ),
        out_shape=[jax.ShapeDtypeStruct((SEG * n, 2 * COLS), F32)]
        + [jax.ShapeDtypeStruct((SEG, KQ), BF16)] * n,
        compiler_params=params(),
        cost_estimate=cost(2 * SEG * n * K * 512, 12 << 20),
    )(yc, *xs, w0, w1, *after)
    return result[0], result[1:]


def quarter_weight(offset):
    return pl.BlockSpec((32, None, 64, COLS), lambda i, yc: (0, (yc[0] + offset(i)) % NY, 0, 0))


def far_kernel(yc, q0, q1, w0, w1, own, near, other, out, stack):
    i = pl.program_id(0)

    @pl.when(i == 0)
    def _():
        out[...] = jnp.zeros_like(out)
        for j, x in enumerate((own, near, other, q0)):
            stack[j] = x[...]

    x = jnp.where(i == 0, q0[...], q1[...])
    out[:, :COLS] += jnp.dot(x, w0[...].reshape(KQ, COLS), preferred_element_type=F32)
    out[:, COLS:] += jnp.dot(x, w1[...].reshape(KQ, COLS), preferred_element_type=F32)


def far_base(yc, q0, q1, w0, w1, quarters):
    weight = quarter_weight(lambda i: i)
    return pl.pallas_call(
        far_kernel,
        grid_spec=pltpu.PrefetchScalarGridSpec(
            num_scalar_prefetch=1,
            grid=(2,),
            in_specs=[whole(SEG, KQ)] * 2 + [weight] * 2 + [whole(SEG, KQ)] * 3,
            out_specs=[whole(SEG, 512), whole(4, SEG, KQ)],
        ),
        out_shape=[
            jax.ShapeDtypeStruct((SEG, 512), F32),
            jax.ShapeDtypeStruct((4, SEG, KQ), BF16),
        ],
        compiler_params=params(),
        cost_estimate=cost(2 * SEG * 2 * KQ * 512, 10 << 20),
    )(yc, q0, q1, w0, w1, *quarters)


def more_kernel(yc, x, w0, w1, before, out):
    x = x[...]
    out[:, :COLS] = before[:, :COLS] + jnp.dot(
        x, w0[...].reshape(KQ, COLS), preferred_element_type=F32
    )
    out[:, COLS:] = before[:, COLS:] + jnp.dot(
        x, w1[...].reshape(KQ, COLS), preferred_element_type=F32
    )


def more_base(yc, x, quarter, w0, w1, before):
    weight = quarter_weight(lambda i: quarter)
    return pl.pallas_call(
        more_kernel,
        grid_spec=pltpu.PrefetchScalarGridSpec(
            num_scalar_prefetch=1,
            grid=(1,),
            in_specs=[whole(SEG, KQ), weight, weight, whole(SEG, 512)],
            out_specs=whole(SEG, 512),
        ),
        out_shape=jax.ShapeDtypeStruct((SEG, 512), F32),
        compiler_params=params(),
        cost_estimate=cost(2 * SEG * KQ * 512, 3 << 20),
    )(yc, x, w0, w1, before)


def whole(*shape):
    return pl.BlockSpec(shape, lambda i, yc: (0,) * len(shape))


def sum_kernel(
    yc, first, second, far, p0, p1, p2, p3, up, out, out_partner, held, sem
):
    me, core = yc[0], yc[1]
    low = (p0[...] + p1[...] + p2[...] + p3[...]).astype(BF16).astype(F32)
    left = lax.broadcasted_iota(jnp.int32, (128, 128), 1) < 64
    copy = pltpu.make_async_copy(held, out.at[:, core], sem)
    for side, columns, to in (
        (core, slice(0, COLS), held),
        (1 - core, slice(COLS, 2 * COLS), out_partner),
    ):
        bases = (first[:SEG, columns], first[SEG:, columns])
        bases += (second[:, columns], far[:, columns])
        for d, base in zip((0, 3 - 2 * core, 1 + 2 * core, 2), bases):
            s = (me + d) & 3
            both = jnp.where(s < 2, low[:SEG], low[SEG:])
            mine = jnp.where(left == (s & 1 == 0), both, 0.0).astype(BF16)
            delta = jnp.dot(mine, up[side, s // 2], preferred_element_type=F32)
            to[s] = (base + delta).astype(BF16)
        if to is held:
            copy.start()
    copy.wait()


def sum_up(yc, first, second, far, parts, up):
    return pl.pallas_call(
        sum_kernel,
        in_specs=[SMEM] + [VMEM] * 8,
        out_specs=[ANY, VMEM],
        out_shape=[
            jax.ShapeDtypeStruct((NY, NC, SEG, COLS), BF16),
            jax.ShapeDtypeStruct((NY, SEG, COLS), BF16),
        ],
        scratch_shapes=[
            pltpu.VMEM((NY, SEG, COLS), BF16),
            pltpu.SemaphoreType.DMA(()),
        ],
        compiler_params=params(),
        cost_estimate=cost(2 * 512 * 128 * 512, 3 << 20),
    )(yc, first, second, far, *parts, up)


def on_device(tokens, weight, down, up, apr, rps):
    y, c = lax.axis_index("y"), lax.axis_index("c")
    yc = jnp.stack([y, c]).astype(jnp.int32)

    send = pack(apr, rps, down, up)
    tokens, send = lax.optimization_barrier((tokens, send))
    near = around(tokens)
    partner_tokens = shift(tokens, "c", 1)
    other = around(partner_tokens, False)
    ahead = ((y + 1 - 2 * c + NY) & 3).reshape(1).astype(jnp.int32)
    q0, q1, q2, q3 = [around(v) for v in split_quarters(ahead, near)]

    recv = lax.all_to_all(send, ("z", "x", "c"), 0, 0)
    weight, _ = lax.optimization_barrier((weight, partner_tokens))
    partner_weight = shift(weight, "c", 1)

    w0 = weight.reshape(32, NY, 64, COLS)
    w1 = partner_weight.reshape(32, NY, 64, COLS)
    first, quarters = near_base(yc, [tokens, near], weight, partner_weight)
    second, more = near_base(yc, [other], weight, partner_weight, (first,))
    far, stack = far_base(yc, q0, q1, w0, w1, [*quarters, *more])

    far = more_base(yc, q2, 2, w0, w1, far)
    parts = low_parts(yc, stack, recv, far)
    far = more_base(yc, q3, 3, in_hbm(w0), in_hbm(w1), far)
    parts = [parts[0]] + [shift(parts[e], "y", e) for e in (1, 2, 3)]
    up_sorted = up_rows(recv)
    out, out_partner = sum_up(yc, first, second, far, parts, up_sorted)
    theirs = shift(out_partner, "c", 1)
    zero = jnp.zeros((), jnp.int32)
    out = lax.dynamic_update_slice(
        out, theirs[:, None], (zero, (1 - c).astype(jnp.int32), zero, zero)
    )
    return out.reshape(NY * NC * SEG, COLS)


def solution(mesh):
    axes = Mesh(mesh.devices.reshape(NZ, NX, NY, NC), ("z", "x", "y", "c"))
    every = ("z", "x", "y", "c")
    placed = (
        P(every, None),
        P(None, ("y", "c")),
        P(None, every, None),
        P(None, ("z", "x"), ("y", "c")),
        P(),
        P(),
    )
    return jax.shard_map(
        on_device,
        mesh=axes,
        in_specs=placed,
        out_specs=P(("z", "x"), ("y", "c")),
        check_vma=False,
    )
```

```python
import functools

import jax
import jax.numpy as jnp
from jax import lax
from jax.experimental import pallas as pl
from jax.experimental.pallas import tpu as pltpu
from jax.sharding import Mesh
from jax.sharding import PartitionSpec as P

NZ, NX, NY, NC = 8, 4, 4, 2
NDP = NZ * NX
SEG = 128
K = 8192
RANK = 64
COLS = 256
KQ = K // NY
BF16, F32 = jnp.bfloat16, jnp.float32
VMEM_LIMIT = 20 * 1024 * 1024
PACK = 8
STEP = 2048
AHEAD = 10**11


def params(**kw):
    return pltpu.CompilerParams(vmem_limit_bytes=VMEM_LIMIT, **kw)


def cost(flops, nbytes):
    return pl.CostEstimate(flops=flops, bytes_accessed=nbytes, transcendentals=0)


def in_hbm(x):
    return pltpu.with_memory_space_constraint(x, pltpu.HBM)


def shift(x, axis, by):
    n = {"y": NY, "c": NC}[axis]
    return lax.ppermute(x, axis, [(i, (i + by) % n) for i in range(n)])


def around(x, to_same_core=True):
    pairs = []
    for y in range(NY):
        for c in range(NC):
            to = (y + 1 - 2 * c) % NY
            pairs.append((y * NC + c, to * NC + (c if to_same_core else 1 - c)))
    return lax.ppermute(x, ("y", "c"), pairs)


def pack_kernel(apr, rps, down_ref, up_ref, out_ref, table, held, sems):
    def fill(a, carry):
        v = up_ref[a].astype(F32)
        table[a] = jnp.concatenate([v[:, :128], v[:, 128:]] * 2, axis=0)
        return carry

    lax.fori_loop(0, 64, fill, 0, unroll=8)
    row = lax.broadcasted_iota(jnp.int32, (8, 128), 0)

    def copy(g):
        part = pl.ds(PACK * g, PACK)
        return pltpu.make_async_copy(held.at[part], out_ref.at[part], sems.at[g])

    for g in range(NDP * NC // PACK):

        def to_device(n, carry):
            first = n // NC * (NY * NC) + n % NC
            ids = [apr[rps[first + s * NC]] for s in range(NY)]
            for s in range(NY):
                held[n, 32 * s : 32 * s + 32, :] = down_ref[ids[s]]
            ups = [
                jnp.where(row < 4, table[ids[s]], table[ids[s + 1]]) for s in (0, 2)
            ]
            held[n, 128:144, :] = jnp.concatenate(ups, axis=0).astype(BF16)
            return carry

        lax.fori_loop(PACK * g, PACK * g + PACK, to_device, 0, unroll=8)
        copy(g).start()
    for g in range(NDP * NC // PACK):
        copy(g).wait()


def pack(apr, rps, down, up):
    return pl.pallas_call(
        pack_kernel,
        in_specs=[
            pl.BlockSpec(memory_space=pltpu.SMEM),
            pl.BlockSpec(memory_space=pltpu.SMEM),
            pl.BlockSpec(memory_space=pltpu.VMEM),
            pl.BlockSpec(memory_space=pltpu.VMEM),
        ],
        out_specs=pl.BlockSpec(memory_space=pl.ANY),
        scratch_shapes=[
            pltpu.VMEM((64, 8, 128), F32),
            pltpu.VMEM((NDP * NC, 144, 128), BF16),
            pltpu.SemaphoreType.DMA((NDP * NC // PACK,)),
        ],
        out_shape=jax.ShapeDtypeStruct((NDP * NC, 144, 128), BF16),
        compiler_params=pltpu.CompilerParams(vmem_limit_bytes=60 * 1024 * 1024),
        cost_estimate=cost(0, 3 << 20),
    )(apr, rps, down, up)


def quarter_of(x_ref, q, pair):
    at = pair * 512 + (q // 2) * 128
    a = x_ref[:, pl.ds(pl.multiple_of(at, 128), 128)]
    b = x_ref[:, pl.ds(pl.multiple_of(at + 256, 128), 128)]
    low = jnp.concatenate([a[:, :64], b[:, :64]], axis=1)
    high = jnp.concatenate([a[:, 64:], b[:, 64:]], axis=1)
    return jnp.where(q % 2 == 0, low, high)


def split_kernel(first, x_ref, *outs):
    for pair in range(16):
        lanes = slice(128 * pair, 128 * pair + 128)
        for i in range(NY):
            outs[i][:, lanes] = quarter_of(x_ref, (first[0] + i) % NY, pair)


def split_quarters(first, x):
    return pl.pallas_call(
        split_kernel,
        grid_spec=pltpu.PrefetchScalarGridSpec(
            num_scalar_prefetch=1,
            grid=(1,),
            in_specs=[pl.BlockSpec((SEG, K), lambda i, *_: (0, 0))],
            out_specs=[pl.BlockSpec((SEG, KQ), lambda i, *_: (0, 0))] * NY,
        ),
        out_shape=[jax.ShapeDtypeStruct((SEG, KQ), BF16)] * NY,
        compiler_params=params(),
        cost_estimate=cost(AHEAD, 4 * SEG * K),
    )(first, x)


def low_kernel(yc, x_ref, recv_ref, after, *rest):
    outs, sums = rest[:NY], rest[NY]
    me, core = yc[0], yc[1]
    for i, d in enumerate((0, 3 - 2 * core, 1 + 2 * core, 2)):
        s = (me + d) & 3
        factor = recv_ref[:, pl.ds(pl.multiple_of(32 * s, 32), 32), :].reshape(KQ, 128)
        sums[s] = jnp.dot(x_ref[i], factor, preferred_element_type=F32)
    lane = lax.broadcasted_iota(jnp.int32, (128, 128), 1)
    for pair in range(2):
        rows = slice(128 * pair, 128 * pair + 128)
        a, b = sums[2 * pair], sums[2 * pair + 1]
        keys = jnp.where(lane < 64, a, pltpu.roll(b, 64, 1))
        values = jnp.where(lane < 64, pltpu.roll(a, 64, 1), b)
        for e in range(NY):
            outs[e][rows, :] = jnp.where(((me + e) & 3) >= 2, values, keys)


SMEM = pl.BlockSpec(memory_space=pltpu.SMEM)
VMEM = pl.BlockSpec(memory_space=pltpu.VMEM)
ANY = pl.BlockSpec(memory_space=pl.ANY)


def low_parts(yc, x, recv, after):
    return pl.pallas_call(
        low_kernel,
        in_specs=[SMEM, VMEM, VMEM, ANY],
        out_specs=[VMEM] * NY,
        scratch_shapes=[pltpu.VMEM((NY, 128, 128), F32)],
        out_shape=[jax.ShapeDtypeStruct((256, 128), F32)] * NY,
        compiler_params=params(),
        cost_estimate=cost(2 * 512 * KQ * 128, 5 << 20),
    )(yc, x, recv, after)


def up_kernel(recv_ref, out_ref):
    r = lax.broadcasted_iota(jnp.int32, (512, 512), 0)
    k = lax.broadcasted_iota(jnp.int32, (512, 512), 1)
    pair, half, seg, rank = r // 256, (r // 128) % 2, (r // 64) % 2, r % 64
    source = (rank // 2) * 16 + (pair * 2 + seg) * 4 + half * 2 + rank % 2
    order = (k == source).astype(F32).astype(BF16)
    every = recv_ref[:, 128:, :].reshape(NDP, NC, 16, 128)
    for c in range(NC):
        rows = every[:, c].reshape(512, 128)
        got = jnp.dot(order, rows, preferred_element_type=F32).astype(BF16)
        for p in range(2):
            for h in range(2):
                at = 256 * p + 128 * h
                out_ref[c, p, :, 128 * h : 128 * h + 128] = got[at : at + 128]


def up_rows(recv):
    return pl.pallas_call(
        up_kernel,
        in_specs=[VMEM],
        out_specs=VMEM,
        out_shape=jax.ShapeDtypeStruct((NC, 2, 128, COLS), BF16),
        compiler_params=params(),
        cost_estimate=cost(2 * 512 * 512 * 256, 1 << 19),
    )(recv)


def near_kernel(n, yc, *refs):
    xs, (w0, w1) = refs[:n], refs[n : n + 2]
    out, quarters = refs[-n - 1], refs[-n:]

    @pl.when(pl.program_id(0) == 0)
    def _():
        out[...] = jnp.zeros_like(out)

    for x, quarter in zip(xs, quarters):
        for pair in range(STEP // 512):
            quarter[:, 128 * pair : 128 * pair + 128] = quarter_of(x, yc[0], pair)
    x = jnp.concatenate([x[...] for x in xs], axis=0)
    out[:, :COLS] += jnp.dot(x, w0[...], preferred_element_type=F32)
    out[:, COLS:] += jnp.dot(x, w1[...], preferred_element_type=F32)


def near_base(yc, xs, w0, w1, after=()):
    step, n = STEP, len(xs)
    weight = pl.BlockSpec((step, COLS), lambda i, yc: (i, 0))
    result = pl.pallas_call(
        functools.partial(near_kernel, n),
        grid_spec=pltpu.PrefetchScalarGridSpec(
            num_scalar_prefetch=1,
            grid=(K // step,),
            in_specs=[pl.BlockSpec((SEG, step), lambda i, yc: (0, i))] * n
            + [weight] * 2
            + [pl.BlockSpec(memory_space=pl.ANY)] * len(after),
            out_specs=[pl.BlockSpec((SEG * n, 2 * COLS), lambda i, yc: (0, 0))]
            + [pl.BlockSpec((SEG, step // NY), lambda i, yc: (0, i))] * n,
        ),
        out_shape=[jax.ShapeDtypeStruct((SEG * n, 2 * COLS), F32)]
        + [jax.ShapeDtypeStruct((SEG, KQ), BF16)] * n,
        compiler_params=params(),
        cost_estimate=cost(2 * SEG * n * K * 512, 12 << 20),
    )(yc, *xs, w0, w1, *after)
    return result[0], result[1:]


def quarter_weight(offset):
    return pl.BlockSpec((32, None, 64, COLS), lambda i, yc: (0, (yc[0] + offset(i)) % NY, 0, 0))


def far_kernel(yc, q0, q1, w0, w1, own, near, other, out, stack):
    i = pl.program_id(0)

    @pl.when(i == 0)
    def _():
        out[...] = jnp.zeros_like(out)
        for j, x in enumerate((own, near, other, q0)):
            stack[j] = x[...]

    x = jnp.where(i == 0, q0[...], q1[...])
    out[:, :COLS] += jnp.dot(x, w0[...].reshape(KQ, COLS), preferred_element_type=F32)
    out[:, COLS:] += jnp.dot(x, w1[...].reshape(KQ, COLS), preferred_element_type=F32)


def far_base(yc, q0, q1, w0, w1, quarters):
    weight = quarter_weight(lambda i: i)
    return pl.pallas_call(
        far_kernel,
        grid_spec=pltpu.PrefetchScalarGridSpec(
            num_scalar_prefetch=1,
            grid=(2,),
            in_specs=[whole(SEG, KQ)] * 2 + [weight] * 2 + [whole(SEG, KQ)] * 3,
            out_specs=[whole(SEG, 512), whole(4, SEG, KQ)],
        ),
        out_shape=[
            jax.ShapeDtypeStruct((SEG, 512), F32),
            jax.ShapeDtypeStruct((4, SEG, KQ), BF16),
        ],
        compiler_params=params(),
        cost_estimate=cost(2 * SEG * 2 * KQ * 512, 10 << 20),
    )(yc, q0, q1, w0, w1, *quarters)


def more_kernel(yc, x, w0, w1, before, out):
    x = x[...]
    out[:, :COLS] = before[:, :COLS] + jnp.dot(
        x, w0[...].reshape(KQ, COLS), preferred_element_type=F32
    )
    out[:, COLS:] = before[:, COLS:] + jnp.dot(
        x, w1[...].reshape(KQ, COLS), preferred_element_type=F32
    )


def more_base(yc, x, quarter, w0, w1, before):
    weight = quarter_weight(lambda i: quarter)
    return pl.pallas_call(
        more_kernel,
        grid_spec=pltpu.PrefetchScalarGridSpec(
            num_scalar_prefetch=1,
            grid=(1,),
            in_specs=[whole(SEG, KQ), weight, weight, whole(SEG, 512)],
            out_specs=whole(SEG, 512),
        ),
        out_shape=jax.ShapeDtypeStruct((SEG, 512), F32),
        compiler_params=params(),
        cost_estimate=cost(2 * SEG * KQ * 512, 3 << 20),
    )(yc, x, w0, w1, before)


def whole(*shape):
    return pl.BlockSpec(shape, lambda i, yc: (0,) * len(shape))


def sum_kernel(
    yc, first, second, far, p0, p1, p2, p3, up, out, out_partner, held, sem
):
    me, core = yc[0], yc[1]
    low = (p0[...] + p1[...] + p2[...] + p3[...]).astype(BF16).astype(F32)
    left = lax.broadcasted_iota(jnp.int32, (128, 128), 1) < 64
    copy = pltpu.make_async_copy(held, out.at[:, core], sem)
    for side, columns, to in (
        (core, slice(0, COLS), held),
        (1 - core, slice(COLS, 2 * COLS), out_partner),
    ):
        bases = (first[:SEG, columns], first[SEG:, columns])
        bases += (second[:, columns], far[:, columns])
        for d, base in zip((0, 3 - 2 * core, 1 + 2 * core, 2), bases):
            s = (me + d) & 3
            both = jnp.where(s < 2, low[:SEG], low[SEG:])
            mine = jnp.where(left == (s & 1 == 0), both, 0.0).astype(BF16)
            delta = jnp.dot(mine, up[side, s // 2], preferred_element_type=F32)
            to[s] = (base + delta).astype(BF16)
        if to is held:
            copy.start()
    copy.wait()


def sum_up(yc, first, second, far, parts, up):
    return pl.pallas_call(
        sum_kernel,
        in_specs=[SMEM] + [VMEM] * 8,
        out_specs=[ANY, VMEM],
        out_shape=[
            jax.ShapeDtypeStruct((NY, NC, SEG, COLS), BF16),
            jax.ShapeDtypeStruct((NY, SEG, COLS), BF16),
        ],
        scratch_shapes=[
            pltpu.VMEM((NY, SEG, COLS), BF16),
            pltpu.SemaphoreType.DMA(()),
        ],
        compiler_params=params(),
        cost_estimate=cost(2 * 512 * 128 * 512, 3 << 20),
    )(yc, first, second, far, *parts, up)


def place_kernel(yc, theirs, _, out, sem):
    copy = pltpu.make_async_copy(theirs, out.at[:, 1 - yc[1]], sem)
    copy.start()
    copy.wait()


def place(yc, theirs, out):
    return pl.pallas_call(
        place_kernel,
        in_specs=[SMEM, VMEM, ANY],
        out_specs=ANY,
        out_shape=jax.ShapeDtypeStruct(out.shape, out.dtype),
        scratch_shapes=[pltpu.SemaphoreType.DMA(())],
        input_output_aliases={2: 0},
        compiler_params=params(),
        cost_estimate=cost(0, 1 << 19),
    )(yc, theirs, out)


def on_device(tokens, weight, down, up, apr, rps):
    y, c = lax.axis_index("y"), lax.axis_index("c")
    yc = jnp.stack([y, c]).astype(jnp.int32)

    send = pack(apr, rps, down, up)
    tokens, send = lax.optimization_barrier((tokens, send))
    near = around(tokens)
    partner_tokens = shift(tokens, "c", 1)
    other = around(partner_tokens, False)
    ahead = ((y + 1 - 2 * c + NY) & 3).reshape(1).astype(jnp.int32)
    q0, q1, q2, q3 = [around(v) for v in split_quarters(ahead, near)]

    recv = lax.all_to_all(send, ("z", "x", "c"), 0, 0)
    weight, _ = lax.optimization_barrier((weight, partner_tokens))
    partner_weight = shift(weight, "c", 1)

    w0 = weight.reshape(32, NY, 64, COLS)
    w1 = partner_weight.reshape(32, NY, 64, COLS)
    first, quarters = near_base(yc, [tokens, near], weight, partner_weight)
    second, more = near_base(yc, [other], weight, partner_weight, (first,))
    far, stack = far_base(yc, q0, q1, w0, w1, [*quarters, *more])

    far = more_base(yc, q2, 2, w0, w1, far)
    parts = low_parts(yc, stack, recv, far)
    far = more_base(yc, q3, 3, in_hbm(w0), in_hbm(w1), far)
    parts = [parts[0]] + [shift(parts[e], "y", e) for e in (1, 2, 3)]
    up_sorted = up_rows(recv)
    out, out_partner = sum_up(yc, first, second, far, parts, up_sorted)
    theirs = shift(out_partner, "c", 1)
    out = place(yc, theirs, out)
    return out.reshape(NY * NC * SEG, COLS)


def solution(mesh):
    axes = Mesh(mesh.devices.reshape(NZ, NX, NY, NC), ("z", "x", "y", "c"))
    every = ("z", "x", "y", "c")
    placed = (
        P(every, None),
        P(None, ("y", "c")),
        P(None, every, None),
        P(None, ("z", "x"), ("y", "c")),
        P(),
        P(),
    )
    return jax.shard_map(
        on_device,
        mesh=axes,
        in_specs=placed,
        out_specs=P(("z", "x"), ("y", "c")),
        check_vma=False,
    )
```
